128 devices in a mesh: dp: 2 (over core), expert: 8 (over x, z_lo), tensor: 8 (over y, z_hi).
Axes of the slice: x: 4, y: 4, z: 4 (z_hi: 2, z_lo: 2; z = z_hi * 2 + z_lo), core: 2. Of those that a mesh axis runs over, the one named last changes fastest.
Arguments:
- tokens: bfloat16 [512, 5120], P(('dp', 'expert'), 'tensor'), may hold values from -50 to 50
- expert_ids: int32 [512, 2], P(('dp', 'expert')), may hold values from 0 to 7, all different within a row; in each aligned block of 32 rows (0 to 31, 32 to 63, ...) at most 16 rows name the same one
- gate_weights: float32 [512, 2], P(('dp', 'expert')), may hold values from 0.1 to 1
- t_gate: bfloat16 [8, 5120, 8192], P('expert', None, ('dp', 'tensor')), may hold values from -0.078125 to 0.078125
- t_up: bfloat16 [8, 5120, 8192], P('expert', None, ('dp', 'tensor')), may hold values from -0.078125 to 0.078125
- t_down: bfloat16 [8, 8192, 5120], P('expert', ('dp', 'tensor')), may hold values from -0.09375 to 0.09375
- s_gate: bfloat16 [5120, 8192], P(None, ('expert', 'tensor')), may hold values from -0.078125 to 0.078125
- s_up: bfloat16 [5120, 8192], P(None, ('expert', 'tensor')), may hold values from -0.078125 to 0.078125
- s_down: bfloat16 [8192, 5120], P(('expert', 'tensor')), may hold values from -0.1875 to 0.1875
Outputs:
- grad_gate: bfloat16 [5120, 8192], P(None, ('expert', 'tensor'))
- grad_up: bfloat16 [5120, 8192], P(None, ('expert', 'tensor'))
- grad_down: bfloat16 [8192, 5120], P(('expert', 'tensor'))
- loss: float32 [], replicated
The draws below stay inside these ranges and needn't reach their ends.
Inputs may be any that keep to these rules, and one draw needn't show every extreme that they name: `expert_ids`: in each aligned block of 32 tokens no expert is named by more than 16 tokens; a token's two experts differ.
All inputs are finite; a program needn't handle non-finite values.
Results may differ from the reference program's by a relative error of at most 0.018.
Values may be sent and summed in bfloat16 or wider, within the bound.
A program may use at most 128 MiB of HBM per device.

```python
import math
import jax
import jax.numpy as jnp
import numpy as np
from jax import lax

D = 5120
FFT = 8192
FFS = 8192
TOK_GRP = 32
EXPERTS = 8
CAP = 16
TOKENS = 512
N_DP = 2
N_TENSOR = 8


def draw_tokens(key, part):
    pieces = jax.random.split(jax.random.fold_in(key, 11), 3)
    positions = jnp.arange(TOKENS, dtype=jnp.float32)
    rising = jnp.exp(0.25 * jnp.log(3.0) * positions / max(TOKENS - 1, 1))
    columns = jnp.exp(jax.random.uniform(pieces[2], (1, D), jnp.float32, jnp.log(0.6), jnp.log(1.6)))
    base = jnp.clip(jax.random.normal(pieces[0], (TOKENS, D), jnp.float32), -6.0, 6.0)
    values = base * rising[:, None] * columns
    return values.astype(jnp.bfloat16)


def with_spikes(array, key, source, target, parts, factor):
    def block_of(dim):
        return (jnp.arange(array.shape[dim]) // (array.shape[dim] // parts)).reshape((-1,) + (1,) * (array.ndim - 1 - dim))

    near = jax.random.permutation(key, parts)[block_of(target)]
    far = (block_of(target) + parts // 2) % parts
    return jnp.where((block_of(source) == near) | (block_of(source) == far), factor * array, array)


def shard_levels(rng, extent, cuts, least, top_value):
    loudness, own = 1.0, jax.random.fold_in(rng, 6)
    for position, parts in cuts:
        steps = jnp.exp(jax.random.uniform(jax.random.fold_in(own, position), (parts,), jnp.float32, least / len(cuts), top_value / len(cuts)))
        loudness = loudness * jnp.repeat(steps, extent[position] // parts).reshape([-1 if axis == position else 1 for axis in range(len(extent))])
    return loudness


def routed_block(stream_key, own, number, rows, number_of, top, limit, skew):
    ranking = jax.random.permutation(stream_key, number_of)
    packed, usual = shares(number_of, rows * top, limit, skew, True), shares(number_of, rows * top, limit, skew, False)
    places = jnp.arange(number_of)

    def named(lengths, rotation):
        used = int((lengths > 0).sum())
        fixed = max(1, used // 4)
        shifted = fixed + (places - fixed + rotation * (used - fixed)) % max(1, number_of - fixed)
        return jnp.zeros((number_of,), jnp.int32).at[ranking[jnp.where(places < fixed, places, shifted)]].set(jnp.asarray(lengths, jnp.int32))

    lengths = jnp.where(number % 4 == 0, named(packed, number // 4), named(usual, number - number // 4 - 1))
    mixed = jax.random.permutation(jax.random.fold_in(own, 3), number_of)
    donor, sink = mixed[0:number_of // 2 * 2:2], mixed[1:number_of // 2 * 2:2]
    room = jnp.minimum(lengths[donor] - 1, limit - lengths[sink]) // 2
    room = jnp.where((donor == ranking[0]) | (sink == ranking[0]) | (lengths[sink] == 0), 0, jnp.maximum(room, 0))
    shifted = jax.random.randint(jax.random.fold_in(own, 4), (number_of // 2,), 0, 1 << 20) % (room + 1)
    lengths = lengths.at[donor].add(-shifted).at[sink].add(shifted)
    items = jnp.searchsorted(jnp.cumsum(lengths), jnp.arange(rows * top), side="right").astype(jnp.int32)
    grid = items.reshape(top, rows).T
    grid = grid[jax.random.permutation(jax.random.fold_in(own, 1), rows)]
    rotation = jax.random.randint(jax.random.fold_in(own, 2), (rows, 1), 0, top)
    return jnp.take_along_axis(grid, (jnp.arange(top)[None, :] + rotation) % top, axis=1)


def shares(count, total, most, lean, full):
    weights = [(1 << 20) // math.isqrt(rank ** lean) + 1 for rank in range(1, count + 1)]
    largest = most if full else min(most, max(-(-total // count), total * weights[0] // sum(weights)))
    least = 1 if total - largest >= count - 1 else 0
    given, spare = [largest] + [least] * (count - 1), total - largest - least * (count - 1)
    while spare > 0:
        movable = [i for i in range(1, count) if given[i] < largest] or [i for i in range(1, count) if given[i] < most]
        whole, remaining = sum([weights[i] for i in movable]), spare
        for i in movable:
            extra = min(most - given[i], max(1, remaining * weights[i] // whole), spare)
            given[i] = given[i] + extra
            spare = spare - extra
    return np.array(given)


def gaussian(key, dims, width, bound, cuts=(), kind=jnp.bfloat16):
    entries = width * jax.random.normal(key, dims, jnp.float32)
    if cuts:
        entries = entries * shard_levels(key, dims, cuts, -0.22, 0.18)
    return jnp.clip(entries, -bound, bound).astype(kind)


def gaussian_with(own_key, extent, scale, reach, cuts, heavy, kind=jnp.bfloat16):
    entries = scale * jax.random.normal(own_key, extent, jnp.float32)
    if cuts:
        entries = entries * shard_levels(own_key, extent, cuts, -0.22, 0.18)
    return jnp.clip(with_spikes(entries, jax.random.fold_in(own_key, 3), *heavy), -reach, reach).astype(kind)


def setup_inputs(seed: int = 0) -> dict:
    key_list = jax.random.split(jax.random.key(seed), 10)
    tokens = draw_tokens(jax.random.fold_in(key_list[9], 71), 0)
    expert_ids_keys = jax.random.split(jax.random.fold_in(key_list[1], 1), TOKENS // TOK_GRP)
    expert_ids_turns = jax.random.permutation(jax.random.fold_in(key_list[1], 3), TOKENS // TOK_GRP)
    expert_ids = jax.vmap(lambda own, number: routed_block(jax.random.fold_in(key_list[1], 2), own, number, TOK_GRP, EXPERTS, 2, CAP, 1))(expert_ids_keys, expert_ids_turns).reshape((TOKENS, 2))
    gate_weights = jnp.clip(jnp.exp(math.log(1.0) - 2.3025851 * jax.random.uniform(key_list[2], (TOKENS, 2), jnp.float32) ** shard_levels(key_list[2], (TOKENS, 2), ((0, 16),), -0.2, 0.2)), 0.1, 1.0)
    t_gate = gaussian(key_list[3], (EXPERTS, D, FFT), D ** -0.5, 0.078125, ((0, 8), (2, 16)))
    t_up = gaussian(key_list[4], (EXPERTS, D, FFT), D ** -0.5, 0.078125, ((0, 8), (2, 16)))
    t_down = gaussian_with(key_list[5], (EXPERTS, FFT, D), FFT ** -0.5, 0.09375, ((0, 8), (1, 16)), (1, 2, 16, 2.0))
    s_gate = gaussian(key_list[6], (D, FFS), D ** -0.5, 0.078125, ((1, 64),))
    s_up = gaussian(key_list[7], (D, FFS), D ** -0.5, 0.078125, ((1, 64),))
    s_down = gaussian_with(key_list[8], (FFS, D), FFS ** -0.5, 0.1875, ((0, 64),), (0, 1, 64, 4.0))
    return dict(tokens=tokens, expert_ids=expert_ids, gate_weights=gate_weights, t_gate=t_gate, t_up=t_up, t_down=t_down, s_gate=s_gate, s_up=s_up, s_down=s_down)


def pair_slots(route_ids):
    flat_ids = route_ids.reshape(-1)
    onehot = (flat_ids[:, None] == jnp.arange(EXPERTS, dtype=jnp.int32)[None, :]).astype(jnp.int32)
    before = jnp.cumsum(onehot, axis=0) - onehot
    slot_rank = lax.optimization_barrier(jnp.sum(before * onehot, axis=1))
    return (flat_ids * CAP + slot_rank).reshape(route_ids.shape)

def reference(tokens, expert_ids, gate_weights, t_gate, t_up, t_down, s_gate, s_up, s_down):
    groups = TOKENS // TOK_GRP
    shards = N_DP * N_TENSOR
    pair_codes = jax.vmap(pair_slots)(expert_ids.reshape(groups, TOK_GRP, 2))
    slot_codes = jnp.arange(EXPERTS * CAP, dtype=jnp.int32)
    group_tokens = tokens.reshape(groups, TOK_GRP, D)

    def dispatch(operands):
        group_x, codes = operands
        placing = lax.optimization_barrier(jnp.sum((codes[None, :, :] == slot_codes[:, None, None]).astype(jnp.float32), axis=2))
        return jnp.dot(placing.astype(jnp.bfloat16), group_x, preferred_element_type=jnp.float32).astype(jnp.bfloat16)
    sent = lax.map(dispatch, (group_tokens, pair_codes))
    expert_rows = sent.reshape(groups, EXPERTS, CAP, D).transpose(1, 0, 2, 3).reshape(EXPERTS, groups * CAP, D)

    def expert_apply(operands):
        rows_in, w_gate, w_up, w_down = operands
        gate_pre = jnp.dot(rows_in, w_gate, preferred_element_type=jnp.float32)
        up_pre = jnp.dot(rows_in, w_up, preferred_element_type=jnp.float32)
        activation = (gate_pre * jax.nn.sigmoid(gate_pre) * up_pre).astype(jnp.bfloat16)
        act_split = activation.reshape(groups * CAP, shards, FFT // shards).transpose(1, 0, 2).astype(jnp.float32)
        down_split = w_down.reshape(shards, FFT // shards, D).astype(jnp.float32)
        partial_value = jnp.einsum('srf,sfd->srd', act_split, down_split)
        rounded = lax.optimization_barrier(partial_value.astype(jnp.bfloat16))
        return lax.optimization_barrier(jnp.sum(rounded.astype(jnp.float32), axis=0)).astype(jnp.bfloat16)
    expert_out = lax.map(expert_apply, (expert_rows, t_gate, t_up, t_down))
    back = expert_out.reshape(EXPERTS, groups, CAP, D).transpose(1, 0, 2, 3).reshape(groups, EXPERTS * CAP, D)
    weighting = gate_weights / lax.optimization_barrier(jnp.sum(gate_weights, axis=1, keepdims=True))
    weighting = weighting.reshape(groups, TOK_GRP, 2)

    def combine(operands):
        codes, weights_here, outputs = operands
        mixing = lax.optimization_barrier(jnp.sum(weights_here[:, :, None] * (codes[:, :, None] == slot_codes[None, None, :]).astype(jnp.float32), axis=1))
        return jnp.dot(mixing, outputs.astype(jnp.float32), precision=lax.Precision.HIGHEST)
    teacher_out = lax.map(combine, (pair_codes, weighting, back)).reshape(TOKENS, D)
    gate_pre = jnp.dot(tokens, s_gate, preferred_element_type=jnp.float32)
    up_pre = jnp.dot(tokens, s_up, preferred_element_type=jnp.float32)
    gate_sig = jax.nn.sigmoid(gate_pre)
    activation = (gate_pre * gate_sig * up_pre).astype(jnp.bfloat16)
    student_out = jnp.dot(activation, s_down, preferred_element_type=jnp.float32)
    residual = student_out - teacher_out
    loss_value = jnp.sum(residual * residual) / (TOKENS * D)
    grad_scale = 1.0 / math.sqrt(TOKENS)
    d_out = (residual * grad_scale).astype(jnp.bfloat16)
    d_act = jnp.dot(d_out, s_down.T, preferred_element_type=jnp.float32)
    d_down = jnp.dot(activation.T, d_out, preferred_element_type=jnp.float32)
    d_gate_pre = (d_act * up_pre * gate_sig * (1.0 + gate_pre * (1.0 - gate_sig))).astype(jnp.bfloat16)
    d_up_pre = (d_act * gate_pre * gate_sig).astype(jnp.bfloat16)
    d_gate = jnp.dot(tokens.T, d_gate_pre, preferred_element_type=jnp.float32)
    d_up = jnp.dot(tokens.T, d_up_pre, preferred_element_type=jnp.float32)
    return (d_gate.astype(jnp.bfloat16), d_up.astype(jnp.bfloat16), d_down.astype(jnp.bfloat16), loss_value)
```

```python
import functools
import math

import jax
import jax.numpy as jnp
from jax import lax
from jax.experimental import pallas as pl
from jax.experimental.pallas import tpu as pltpu
from jax.sharding import Mesh
from jax.sharding import PartitionSpec as P

MESH = pl.DeviceIdType.MESH
AXES = ("dp", "x", "zl", "y", "zh")
D, ROWS, COLS, HID, SHID, TOKENS = 5120, 32, 640, 512, 128, 512
PARTS = ((0, 256, "yzx"), (256, 256, "zxy"), (512, 128, "xyz"))
GROUPS = (2, 1, 3, 0)
F32, BF16 = jnp.float32, jnp.bfloat16


def coords():
    c = {a: lax.axis_index(a) for a in AXES}
    c["z"] = c["zh"] * 2 + c["zl"]
    return c


def dev(axis, v):
    return {"zh": v // 2, "zl": v % 2} if axis == "z" else {axis: v}


def region(c, dp=None, rows=(0, ROWS), **fixed):
    at = {a: fixed.get(a, c[a]) for a in "xyz"}
    sl = {a: pl.ds(0, 4) if at[a] is None else pl.ds(at[a], 1) for a in "xy"}
    if at["z"] is None:
        zh = zl = pl.ds(0, 2)
    else:
        zh, zl = pl.ds(at["z"] // 2, 1), pl.ds(at["z"] % 2, 1)
    head = (sl["y"], zh) if dp is None else (sl["y"], zh, pl.ds(dp, 1))
    return (*head, sl["x"], zl, pl.ds(*rows))


class Links:
    def __init__(self, send_sem, recv_sem):
        self.ss, self.rs, self.n, self.started = send_sem, recv_sem, 0, []

    def number(self):
        self.n += 1
        return self.n - 1

    def copy(self, src, dst, to, k):
        return pltpu.make_async_remote_copy(
            src_ref=src, dst_ref=dst, send_sem=self.ss.at[k], recv_sem=self.rs.at[k], device_id=to, device_id_type=MESH
        )

    def send(self, src, dst, to, k):
        cp = self.copy(src, dst, to, k)
        cp.start()
        self.started.append(cp)

    def wait(self, dst, to, k):
        self.copy(dst, dst, to, k).wait_recv()

    def finish(self):
        for cp in self.started:
            cp.wait_send()


class Gather:
    def __init__(self, c, links, X, axes):
        self.c, self.ln, self.X = c, links, X
        self.a1, self.a2, self.a3 = axes
        self.k1 = [links.number() for _ in range(3)]
        self.k2 = [links.number() for _ in range(3)]
        self.k3 = [[links.number() for _ in range(4)] for _ in range(4)]
        self.kd = [links.number() for _ in range(4)]
        self.r, self.l, self.o = (c[self.a3] + 1) % 4, (c[self.a3] + 3) % 4, (c[self.a3] + 2) % 4

    def at(self, rows=(0, ROWS), dp=None, **fixed):
        return self.X.at[region(self.c, self.c["dp"] if dp is None else dp, rows, **fixed)]

    def peer(self, axis, s):
        return dev(axis, (self.c[axis] + s) % 4)

    def start1(self):
        for s in (1, 3, 2):
            self.ln.send(self.at(), self.at(), self.peer(self.a1, s), self.k1[s - 1])

    def start2(self):
        c = self.c
        for s in (1, 2, 3):
            self.ln.wait(self.at(**{self.a1: (c[self.a1] + 4 - s) % 4}), self.peer(self.a1, s), self.k1[s - 1])
        for s in (1, 3, 2):
            ref = self.at(**{self.a1: None})
            self.ln.send(ref, ref, self.peer(self.a2, s), self.k2[s - 1])
        self.ring1(0)

    def block(self, k, v3, rows=(0, ROWS)):
        return self.at(rows, **{self.a1: None, self.a2: (self.c[self.a2] + 4 - k) % 4, self.a3: v3})

    def ring1(self, k):
        if k:
            self.ln.wait(self.block(k, self.c[self.a3]), self.peer(self.a2, k), self.k2[k - 1])
        ref = self.block(k, self.c[self.a3])
        self.ln.send(ref, ref, dev(self.a3, self.r), self.k3[k][0])
        self.ln.send(ref, ref, dev(self.a3, self.l), self.k3[k][1])

    def ring2(self, k):
        self.ln.wait(self.block(k, self.l), dev(self.a3, self.r), self.k3[k][0])
        ref = self.block(k, self.l, (0, 16))
        self.ln.send(ref, ref, dev(self.a3, self.r), self.k3[k][2])
        self.ln.wait(self.block(k, self.r), dev(self.a3, self.l), self.k3[k][1])
        ref = self.block(k, self.r, (16, 16))
        self.ln.send(ref, ref, dev(self.a3, self.l), self.k3[k][3])

    def ring3(self, k):
        self.ln.wait(self.block(k, self.o, (0, 16)), dev(self.a3, self.r), self.k3[k][2])
        self.ln.wait(self.block(k, self.o, (16, 16)), dev(self.a3, self.l), self.k3[k][3])

    def plane(self, s, dp=None):
        return self.at(dp=dp, **{self.a1: None, self.a2: None, self.a3: (self.c[self.a3] + s) % 4})

    def across(self, s):
        self.ln.send(self.plane(s), self.plane(s), {"dp": 1 - self.c["dp"]}, self.kd[s])

    def crossed(self):
        for s in (0, 1, 3, 2):
            self.ln.wait(self.plane(s, 1 - self.c["dp"]), {"dp": 1 - self.c["dp"]}, self.kd[s])


def gather_rest(parts):
    for g in parts:
        g.ring2(0)
    for k in (1, 3, 2):
        for g in parts:
            g.ring1(k)
    for g in parts:
        g.across(0)
    for k in (1, 3, 2):
        for g in parts:
            g.ring2(k)
    for g in parts:
        g.across(1)
        g.across(3)
    for g in parts:
        for k in (0, 1, 3, 2):
            g.ring3(k)
        g.across(2)


class Reduce:
    def __init__(self, c, links, sums, got1, got2, got3, axes):
        self.c, self.ln, self.S, self.g1, self.g2, self.g3 = c, links, sums, got1, got2, got3
        self.a1, self.a2, self.a3 = axes
        self.k1 = [[links.number() for _ in range(6)] for _ in range(4)]
        self.k2 = [links.number() for _ in range(3)]
        self.k3 = [links.number() for _ in range(3)]
        self.r, self.l, self.o = (c[self.a3] + 1) % 4, (c[self.a3] + 3) % 4, (c[self.a3] + 2) % 4

    def idx(self, k, v3, rows=(0, ROWS)):
        v2 = (self.c[self.a2] + GROUPS[k]) % 4
        return region(self.c, None, rows, **{self.a1: None, self.a2: v2, self.a3: v3})

    def right(self, k, j, src):
        self.ln.send(src, self.g1.at[k, j], dev(self.a3, self.r), self.k1[k][j])

    def left(self, k, j, src):
        self.ln.send(src, self.g1.at[k, j], dev(self.a3, self.l), self.k1[k][j])

    def got(self, k, j):
        self.ln.wait(self.g1.at[k, j], dev(self.a3, self.r if j < 3 else self.l), self.k1[k][j])
        return self.g1[k, j].astype(F32)

    def ring1(self, k):
        S = self.S
        self.right(k, 0, S.at[self.idx(k, self.o, (0, 16))])
        self.left(k, 3, S.at[self.idx(k, self.o, (16, 16))])
        self.right(k, 1, S.at[self.idx(k, self.r, (16, 16))])
        self.left(k, 4, S.at[self.idx(k, self.l, (0, 16))])

    def ring2(self, k):
        S = self.S
        i = self.idx(k, self.r, (0, 16))
        S[i] = (S[i].astype(F32) + self.got(k, 0)).astype(BF16)
        self.right(k, 2, S.at[i])
        i = self.idx(k, self.l, (16, 16))
        S[i] = (S[i].astype(F32) + self.got(k, 3)).astype(BF16)
        self.left(k, 5, S.at[i])

    def ring3(self, k):
        S, own = self.S, self.c[self.a3]
        i = self.idx(k, own, (0, 16))
        S[i] = (S[i].astype(F32) + self.got(k, 4) + self.got(k, 2)).astype(BF16)
        i = self.idx(k, own, (16, 16))
        S[i] = (S[i].astype(F32) + self.got(k, 1) + self.got(k, 5)).astype(BF16)
        s = GROUPS[k]
        if s:
            to = dev(self.a2, (self.c[self.a2] + s) % 4)
            self.ln.send(S.at[self.idx(k, own)], self.g2.at[s - 1], to, self.k2[s - 1])

    def second(self):
        S = self.S
        i = region(self.c, **{self.a1: None})
        total = S[i].astype(F32)
        for s in (1, 2, 3):
            self.ln.wait(self.g2.at[s - 1], dev(self.a2, (self.c[self.a2] + s) % 4), self.k2[s - 1])
            total = total + self.g2[s - 1].astype(F32)
        S[i] = total.astype(BF16)
        for s in (1, 3, 2):
            v1 = (self.c[self.a1] + s) % 4
            self.ln.send(S.at[region(self.c, **{self.a1: v1})], self.g3.at[s - 1], dev(self.a1, v1), self.k3[s - 1])

    def third(self):
        total = self.S[region(self.c)].astype(F32)
        for s in (1, 2, 3):
            self.ln.wait(self.g3.at[s - 1], dev(self.a1, (self.c[self.a1] + s) % 4), self.k3[s - 1])
            total = total + self.g3[s - 1].astype(F32)
        return total


def wide(refs, y, zh):
    return jnp.concatenate([r[y, zh].reshape(TOKENS, r.shape[-1]) for r in refs], axis=1)


def kernel(tok, ids, gw, tg, tu, td, sg, su, sd, gg, gu, gd, loss, *scratch):
    X, Dx, S, R1, R2, R3 = (scratch[3 * i : 3 * i + 3] for i in range(6))
    W, WD, acc, acts, stage, sact, dcat, wt, lb, ss, rs, lsem = scratch[18:]
    c = coords()
    dp = c["dp"]
    other = {"dp": 1 - dp}
    expert = c["x"] * 2 + c["zl"]

    loads = [
        pltpu.make_async_copy(tg.at[0], W.at[:, pl.ds(0, HID)], lsem.at[0]),
        pltpu.make_async_copy(tu.at[0], W.at[:, pl.ds(HID, HID)], lsem.at[1]),
        pltpu.make_async_copy(sg, W.at[:, pl.ds(2 * HID, SHID)], lsem.at[2]),
        pltpu.make_async_copy(su, W.at[:, pl.ds(2 * HID + SHID, SHID)], lsem.at[3]),
        pltpu.make_async_copy(td.at[0], WD.at[pl.ds(dp * HID, HID)], lsem.at[4]),
        pltpu.make_async_copy(sd, WD.at[pl.ds(2 * HID, SHID)], lsem.at[5]),
    ]

    bar = pltpu.get_barrier_semaphore()
    for a in "xyz":
        for s in (1, 2, 3):
            pl.semaphore_signal(bar, inc=1, device_id=dev(a, (c[a] + s) % 4), device_id_type=MESH)
    pl.semaphore_signal(bar, inc=1, device_id=other, device_id_type=MESH)

    own = region(c, dp)
    for x, (first, width, _) in zip(X, PARTS):
        x[own] = tok[:, first : first + width][None, None, None, None, None]
    lane = lax.broadcasted_iota(jnp.int32, (ROWS, 128), 1)
    norm = gw[...] / jnp.sum(gw[...], axis=1, keepdims=True)
    weight = jnp.where(lane == ids[:, 0:1], norm[:, 0:1], 0.0) + jnp.where(lane == ids[:, 1:2], norm[:, 1:2], 0.0)
    wt[pl.ds(dp, 1), pl.ds(c["x"], 1), pl.ds(c["zl"], 1)] = weight[None, None, None]

    pl.semaphore_wait(bar, 10)
    ln = Links(ss, rs)
    parts = [Gather(c, ln, x, axes) for x, (_, _, axes) in zip(X, PARTS)]
    for g in parts:
        g.start1()
    for cp in loads:
        cp.start()

    k_td, k_h, k_zl, k_wd = (ln.number() for _ in range(4))
    k_wx = [ln.number() for _ in range(3)]
    mine = wt.at[pl.ds(dp, 1), pl.ds(c["x"], 1), pl.ds(c["zl"], 1)]
    pair = wt.at[pl.ds(dp, 1), pl.ds(c["x"], 1)]
    ln.send(mine, mine, {"zl": 1 - c["zl"]}, k_zl)
    ln.send(td.at[0], WD.at[pl.ds(dp * HID, HID)], other, k_td)
    for g in parts:
        g.start2()
    ln.wait(wt.at[pl.ds(dp, 1), pl.ds(c["x"], 1), pl.ds(1 - c["zl"], 1)], {"zl": 1 - c["zl"]}, k_zl)
    for s in (1, 2, 3):
        ln.send(pair, pair, dev("x", (c["x"] + s) % 4), k_wx[s - 1])
    gather_rest(parts)
    for s in (1, 2, 3):
        ln.wait(wt.at[pl.ds(dp, 1), pl.ds((c["x"] + 4 - s) % 4, 1)], dev("x", (c["x"] + s) % 4), k_wx[s - 1])
    ln.send(wt.at[pl.ds(dp, 1)], wt.at[pl.ds(dp, 1)], other, k_wd)
    for cp in loads:
        cp.wait()
    for g in parts:
        g.crossed()
    ln.wait(wt.at[pl.ds(1 - dp, 1)], other, k_wd)

    def up_step(i, carry):
        y, n = i // 5, i % 5
        rows = jnp.concatenate([wide(X, y, 0), wide(X, y, 1)], axis=1)
        cols = pl.ds(pl.multiple_of(n * 256, 256), 256)
        w = W[pl.ds(pl.multiple_of(y * 1280, 1280), 1280), cols]
        part = jnp.dot(rows, w, preferred_element_type=F32)

        @pl.when(y == 0)
        def _():
            acc[:, cols] = part

        @pl.when(y > 0)
        def _():
            acc[:, cols] += part

        return carry

    lax.fori_loop(0, 20, up_step, 0)

    lane = lax.broadcasted_iota(jnp.int32, (128, 128), 1)

    def act_step(i, carry):
        half = (1 - dp + i // 2) % 2
        r0 = pl.multiple_of(half * 256 + (i % 2) * 128, 128)
        rows = pl.ds(r0, 128)
        w4 = wt[half, pl.ds((i % 2) * 2, 2)].reshape(128, 128)
        w = jnp.sum(jnp.where(lane == expert, w4, 0.0), axis=1, keepdims=True)
        g, u = acc[rows, 0:HID], acc[rows, HID : 2 * HID]
        h = (g * jax.nn.sigmoid(g) * u * (-w)).astype(BF16)
        to = pl.ds(pl.multiple_of((i % 2) * 128, 128), 128)
        g, u = acc[rows, 2 * HID : 2 * HID + SHID], acc[rows, 2 * HID + SHID :]
        a = (g * jax.nn.sigmoid(g) * u).astype(BF16)
        sact[rows] = a

        @pl.when(i < 2)
        def _():
            stage[to] = h

        @pl.when(i >= 2)
        def _():
            acts[to, pl.ds(pl.multiple_of(dp * HID, HID), HID)] = h
            acts[to, 2 * HID :] = a

        return carry

    lax.fori_loop(0, 2, act_step, 0)
    there = acts.at[:, pl.ds(pl.multiple_of(dp * HID, HID), HID)]
    ln.send(stage, there, other, k_h)
    lax.fori_loop(2, 4, act_step, 0)
    ln.wait(WD.at[pl.ds((1 - dp) * HID, HID)], other, k_td)
    ln.wait(acts.at[:, pl.ds(pl.multiple_of((1 - dp) * HID, HID), HID)], other, k_h)

    reduces = [Reduce(c, ln, *refs, axes) for *refs, (_, _, axes) in zip(S, R1, R2, R3, PARTS)]
    for red, (first, width, _) in zip(reduces, PARTS):

        def down_step(t, carry):
            w = WD[:, pl.ds(pl.multiple_of(t * COLS + first, 128), width)]
            part = jnp.dot(acts[...], w, preferred_element_type=F32).astype(BF16)
            red.S[t // 2, t % 2] = part.reshape(4, 2, ROWS, width)
            return carry

        lax.fori_loop(0, 8, down_step, 0)
        for k in range(4):
            red.ring1(k)

    def turn(y, carry):
        for zh in range(2):
            for x, (first, width, _) in zip(X, PARTS):
                rows = pl.ds(pl.multiple_of(y * 1280 + zh * COLS + first, 128), width)
                W[rows, 0:TOKENS] = x[y, zh].reshape(TOKENS, width).T
        return carry

    lax.fori_loop(0, 4, turn, 0)

    for k in range(5):
        for red in reduces:
            if k < 4:
                red.ring2(k)
        for red in reduces:
            if k > 0:
                red.ring3(k - 1)
    for red in reduces:
        red.second()
    grads = [Gather(c, ln, x, axes) for x, (_, _, axes) in zip(Dx, PARTS)]
    squares = jnp.zeros((8, 128), F32)
    for red, g, (_, width, _) in zip(reduces, grads, PARTS):
        res = red.third()
        g.X[own] = (res * (1.0 / math.sqrt(TOKENS))).astype(BF16)[:, :, None]
        g.start1()
        sq = res.reshape(4, 8, width)
        sq = jnp.sum(sq * sq, axis=0)
        for j in range(width // 128):
            squares = squares + sq[:, 128 * j : 128 * j + 128]

    def loss_send(n, axis, value):
        k = [ln.number() for _ in range(3)]
        lb[n, pl.ds(c[axis], 1)] = value[None]
        count = 2 if axis == "dp" else 4
        mine = lb.at[n, pl.ds(c[axis], 1)]
        peers = [(s, (c[axis] + s) % count, (c[axis] + count - s) % count) for s in range(1, count)]
        for s, to, _ in peers:
            ln.send(mine, mine, dev(axis, to), k[s - 1])
        return n, axis, peers, k

    def loss_wait(sent):
        n, axis, peers, k = sent
        for s, to, source in peers:
            ln.wait(lb.at[n, pl.ds(source, 1)], dev(axis, to), k[s - 1])
        total = lb[n, 0] + lb[n, 1]
        return total if axis == "dp" else total + lb[n, 2] + lb[n, 3]

    sent = loss_send(0, "x", squares)
    for g in grads:
        g.start2()
    sent = loss_send(1, "y", loss_wait(sent))
    gather_rest(grads)
    sent = loss_send(2, "z", loss_wait(sent))
    sent = loss_send(3, "dp", loss_wait(sent))
    for g in grads:
        g.crossed()

    def dact_step(t, total):
        cols = pl.ds(pl.multiple_of(t * COLS, 128), COLS)
        w = WD[pl.ds(2 * HID, SHID), cols]
        d = wide(Dx, t // 2, t % 2)
        acc[:, 0:SHID] += lax.dot_general(d, w, (((1,), (1,)), ((), ())), preferred_element_type=F32)
        return total

    acc[:, 0:SHID] = jnp.zeros((TOKENS, SHID), F32)
    lax.fori_loop(0, 8, dact_step, 0)
    g, u, da = acc[:, 2 * HID : 2 * HID + SHID], acc[:, 2 * HID + SHID :], acc[:, 0:SHID]
    s = jax.nn.sigmoid(g)
    dcat[:, 0:SHID] = (da * u * s * (1.0 + g * (1.0 - s))).astype(BF16)
    dcat[:, SHID:] = (da * g * s).astype(BF16)

    def grad_step(t, carry):
        rows = pl.ds(pl.multiple_of(t * COLS, 128), COLS)
        both = jnp.dot(W[rows, 0:TOKENS], dcat[...], preferred_element_type=F32).astype(BF16)
        gg[rows] = both[:, :SHID]
        gu[rows] = both[:, SHID:]
        d = wide(Dx, t // 2, t % 2)
        gd[:, rows] = lax.dot_general(
            sact[...], d, (((0,), (0,)), ((), ())), preferred_element_type=F32
        ).astype(BF16)
        return carry

    lax.fori_loop(0, 8, grad_step, 0)
    loss[...] = jnp.full((8, 128), jnp.sum(loss_wait(sent)) / (TOKENS * D), F32)
    ln.finish()


def body(*args):
    vmem, hbm = pl.BlockSpec(memory_space=pltpu.VMEM), pl.BlockSpec(memory_space=pl.ANY)
    blocks = {"x": (1, 1, 4, 1), "y": (4, 1, 1, 1), "z": (1, 2, 1, 2)}
    whole = [pltpu.VMEM((4, 2, 2, 4, 2, ROWS, w), BF16) for _, w, _ in PARTS]
    gg, gu, gd, loss = pl.pallas_call(
        kernel,
        out_shape=(
            jax.ShapeDtypeStruct((D, SHID), BF16),
            jax.ShapeDtypeStruct((D, SHID), BF16),
            jax.ShapeDtypeStruct((SHID, D), BF16),
            jax.ShapeDtypeStruct((8, 128), F32),
        ),
        in_specs=[vmem] * 3 + [hbm] * 6,
        out_specs=(vmem,) * 4,
        scratch_shapes=[
            *whole,
            *whole,
            *[pltpu.VMEM((4, 2, 4, 2, ROWS, w), BF16) for _, w, _ in PARTS],
            *[pltpu.VMEM((4, 6, *blocks[a[0]], 16, w), BF16) for _, w, a in PARTS],
            *[pltpu.VMEM((3, *blocks[a[0]], ROWS, w), BF16) for _, w, a in PARTS],
            *[pltpu.VMEM((3, 1, 1, 1, 1, ROWS, w), BF16) for _, w, _ in PARTS],
            pltpu.VMEM((D, 2 * HID + 2 * SHID), BF16),
            pltpu.VMEM((2 * HID + SHID, D), BF16),
            pltpu.VMEM((TOKENS, 2 * HID + 2 * SHID), F32),
            pltpu.VMEM((TOKENS // 2, 2 * HID + SHID), BF16),
            pltpu.VMEM((TOKENS // 2, HID), BF16),
            pltpu.VMEM((TOKENS, SHID), BF16),
            pltpu.VMEM((TOKENS, 2 * SHID), BF16),
            pltpu.VMEM((2, 4, 2, ROWS, 128), F32),
            pltpu.VMEM((4, 4, 8, 128), F32),
            pltpu.SemaphoreType.DMA((300,)),
            pltpu.SemaphoreType.DMA((300,)),
            pltpu.SemaphoreType.DMA((6,)),
        ],
        compiler_params=pltpu.CompilerParams(
            collective_id=0, has_side_effects=True, vmem_limit_bytes=60 * 2**20
        ),
    )(*args)
    return gg, gu, gd, loss[0, 0]


def solution(mesh):
    finer = Mesh(mesh.devices.reshape(2, 4, 2, 4, 2), AXES)
    rows, tensor, expert = ("dp", "x", "zl"), ("y", "zh"), ("x", "zl")
    hidden, shards = ("dp", "y", "zh"), ("x", "zl", "y", "zh")
    return jax.shard_map(
        body,
        mesh=finer,
        in_specs=(
            P(rows, tensor),
            P(rows, None),
            P(rows, None),
            P(expert, None, hidden),
            P(expert, None, hidden),
            P(expert, hidden, None),
            P(None, shards),
            P(None, shards),
            P(shards, None),
        ),
        out_specs=(P(None, shards), P(None, shards), P(shards, None), P()),
        check_vma=False,
    )
```

```python
import functools
import math

import jax
import jax.numpy as jnp
from jax import lax
from jax.experimental import pallas as pl
from jax.experimental.pallas import tpu as pltpu
from jax.sharding import Mesh
from jax.sharding import PartitionSpec as P

MESH = pl.DeviceIdType.MESH
AXES = ("dp", "x", "zl", "y", "zh")
D, ROWS, COLS, HID, SHID, TOKENS = 5120, 32, 640, 512, 128, 512
PARTS = ((0, 256, "yzx"), (256, 256, "zxy"), (512, 128, "xyz"))
GROUPS = (2, 1, 3, 0)
F32, BF16 = jnp.float32, jnp.bfloat16


def coords():
    c = {a: lax.axis_index(a) for a in AXES}
    c["z"] = c["zh"] * 2 + c["zl"]
    return c


def dev(axis, v):
    return {"zh": v // 2, "zl": v % 2} if axis == "z" else {axis: v}


def region(c, dp=None, rows=(0, ROWS), **fixed):
    at = {a: fixed.get(a, c[a]) for a in "xyz"}
    sl = {a: pl.ds(0, 4) if at[a] is None else pl.ds(at[a], 1) for a in "xy"}
    if at["z"] is None:
        zh = zl = pl.ds(0, 2)
    else:
        zh, zl = pl.ds(at["z"] // 2, 1), pl.ds(at["z"] % 2, 1)
    head = (sl["y"], zh) if dp is None else (sl["y"], zh, pl.ds(dp, 1))
    return (*head, sl["x"], zl, pl.ds(*rows))


class Links:
    def __init__(self, send_sem, recv_sem):
        self.ss, self.rs, self.n, self.started = send_sem, recv_sem, 0, []

    def number(self):
        self.n += 1
        return self.n - 1

    def copy(self, src, dst, to, k):
        return pltpu.make_async_remote_copy(
            src_ref=src, dst_ref=dst, send_sem=self.ss.at[k], recv_sem=self.rs.at[k], device_id=to, device_id_type=MESH
        )

    def send(self, src, dst, to, k):
        cp = self.copy(src, dst, to, k)
        cp.start()
        self.started.append(cp)

    def wait(self, dst, to, k):
        self.copy(dst, dst, to, k).wait_recv()

    def finish(self):
        for cp in self.started:
            cp.wait_send()


class Gather:
    def __init__(self, c, links, X, axes):
        self.c, self.ln, self.X = c, links, X
        self.a1, self.a2, self.a3 = axes
        self.k1 = [links.number() for _ in range(3)]
        self.k2 = [links.number() for _ in range(3)]
        self.k3 = [[links.number() for _ in range(4)] for _ in range(4)]
        self.kd = [links.number() for _ in range(4)]
        self.ko = [links.number() for _ in range(4)]
        self.r, self.l, self.o = (c[self.a3] + 1) % 4, (c[self.a3] + 3) % 4, (c[self.a3] + 2) % 4

    def at(self, rows=(0, ROWS), dp=None, **fixed):
        return self.X.at[region(self.c, self.c["dp"] if dp is None else dp, rows, **fixed)]

    def peer(self, axis, s):
        return dev(axis, (self.c[axis] + s) % 4)

    def start1(self):
        for s in (1, 3, 2):
            self.ln.send(self.at(), self.at(), self.peer(self.a1, s), self.k1[s - 1])

    def start2(self):
        c = self.c
        for s in (1, 2, 3):
            self.ln.wait(self.at(**{self.a1: (c[self.a1] + 4 - s) % 4}), self.peer(self.a1, s), self.k1[s - 1])
        for s in (1, 3, 2):
            ref = self.at(**{self.a1: None})
            self.ln.send(ref, ref, self.peer(self.a2, s), self.k2[s - 1])
        self.ring1(0)

    def block(self, k, v3, rows=(0, ROWS)):
        return self.at(rows, **{self.a1: None, self.a2: (self.c[self.a2] + 4 - k) % 4, self.a3: v3})

    def ring1(self, k):
        if k:
            self.ln.wait(self.block(k, self.c[self.a3]), self.peer(self.a2, k), self.k2[k - 1])
        ref = self.block(k, self.c[self.a3])
        self.ln.send(ref, ref, dev(self.a3, self.r), self.k3[k][0])
        self.ln.send(ref, ref, dev(self.a3, self.l), self.k3[k][1])

    def ring2(self, k):
        self.ln.wait(self.block(k, self.l), dev(self.a3, self.r), self.k3[k][0])
        ref = self.block(k, self.l, (0, 16))
        self.ln.send(ref, ref, dev(self.a3, self.r), self.k3[k][2])
        self.ln.wait(self.block(k, self.r), dev(self.a3, self.l), self.k3[k][1])
        ref = self.block(k, self.r, (16, 16))
        self.ln.send(ref, ref, dev(self.a3, self.l), self.k3[k][3])

    def ring3(self, k):
        self.ln.wait(self.block(k, self.o, (0, 16)), dev(self.a3, self.r), self.k3[k][2])
        self.ln.wait(self.block(k, self.o, (16, 16)), dev(self.a3, self.l), self.k3[k][3])
        ref = self.block(k, self.o)
        self.ln.send(ref, ref, {"dp": 1 - self.c["dp"]}, self.ko[k])

    def plane(self, s, dp=None):
        return self.at(dp=dp, **{self.a1: None, self.a2: None, self.a3: (self.c[self.a3] + s) % 4})

    def across(self, s):
        self.ln.send(self.plane(s), self.plane(s), {"dp": 1 - self.c["dp"]}, self.kd[s])

    def crossed(self, s):
        dp = 1 - self.c["dp"]
        if s == 2:
            for k in (0, 1, 3, 2):
                at = {self.a1: None, self.a2: (self.c[self.a2] + 4 - k) % 4, self.a3: self.o}
                self.ln.wait(self.at(dp=dp, **at), {"dp": dp}, self.ko[k])
        else:
            self.ln.wait(self.plane(s, dp), {"dp": dp}, self.kd[s])
        return (self.c[self.a3] + s) % 4


def gather_rest(parts, use):
    for g in parts:
        g.ring2(0)
    for k in (1, 3, 2):
        for g in parts:
            g.ring1(k)
    for g in parts:
        g.across(0)
    for i in (0, 1):
        use(i, parts[i].crossed(0))
    for g in parts:
        g.ring2(1)
    use(2, parts[2].crossed(0))
    for g in parts:
        g.ring2(3)
    for g in parts:
        g.ring2(2)
        g.across(1)
        g.across(3)
    for i, g in enumerate(parts):
        use(i, g.crossed(1))
    for k in (0, 1, 3, 2):
        for g in parts:
            g.ring3(k)
    for s in (3, 2):
        for i, g in enumerate(parts):
            use(i, g.crossed(s))


class Reduce:
    def __init__(self, c, links, sums, got1, got2, got3, axes):
        self.c, self.ln, self.S, self.g1, self.g2, self.g3 = c, links, sums, got1, got2, got3
        self.a1, self.a2, self.a3 = axes
        self.k1 = [[links.number() for _ in range(6)] for _ in range(4)]
        self.k2 = [links.number() for _ in range(3)]
        self.k3 = [links.number() for _ in range(3)]
        self.r, self.l, self.o = (c[self.a3] + 1) % 4, (c[self.a3] + 3) % 4, (c[self.a3] + 2) % 4

    def idx(self, k, v3, rows=(0, ROWS)):
        v2 = (self.c[self.a2] + GROUPS[k]) % 4
        return region(self.c, None, rows, **{self.a1: None, self.a2: v2, self.a3: v3})

    def right(self, k, j, src):
        self.ln.send(src, self.g1.at[k, j], dev(self.a3, self.r), self.k1[k][j])

    def left(self, k, j, src):
        self.ln.send(src, self.g1.at[k, j], dev(self.a3, self.l), self.k1[k][j])

    def got(self, k, j):
        self.ln.wait(self.g1.at[k, j], dev(self.a3, self.r if j < 3 else self.l), self.k1[k][j])
        return self.g1[k, j].astype(F32)

    def ring1(self, k):
        S = self.S
        self.right(k, 0, S.at[self.idx(k, self.o, (0, 16))])
        self.left(k, 3, S.at[self.idx(k, self.o, (16, 16))])
        self.right(k, 1, S.at[self.idx(k, self.r, (16, 16))])
        self.left(k, 4, S.at[self.idx(k, self.l, (0, 16))])

    def ring2(self, k):
        S = self.S
        i = self.idx(k, self.r, (0, 16))
        S[i] = (S[i].astype(F32) + self.got(k, 0)).astype(BF16)
        self.right(k, 2, S.at[i])
        i = self.idx(k, self.l, (16, 16))
        S[i] = (S[i].astype(F32) + self.got(k, 3)).astype(BF16)
        self.left(k, 5, S.at[i])

    def ring3(self, k):
        S, own = self.S, self.c[self.a3]
        i = self.idx(k, own, (0, 16))
        S[i] = (S[i].astype(F32) + self.got(k, 4) + self.got(k, 2)).astype(BF16)
        i = self.idx(k, own, (16, 16))
        S[i] = (S[i].astype(F32) + self.got(k, 1) + self.got(k, 5)).astype(BF16)
        s = GROUPS[k]
        if s:
            to = dev(self.a2, (self.c[self.a2] + s) % 4)
            self.ln.send(S.at[self.idx(k, own)], self.g2.at[s - 1], to, self.k2[s - 1])

    def second(self):
        S = self.S
        i = region(self.c, **{self.a1: None})
        total = S[i].astype(F32)
        for s in (1, 2, 3):
            self.ln.wait(self.g2.at[s - 1], dev(self.a2, (self.c[self.a2] + s) % 4), self.k2[s - 1])
            total = total + self.g2[s - 1].astype(F32)
        S[i] = total.astype(BF16)
        for s in (1, 3, 2):
            v1 = (self.c[self.a1] + s) % 4
            self.ln.send(S.at[region(self.c, **{self.a1: v1})], self.g3.at[s - 1], dev(self.a1, v1), self.k3[s - 1])

    def third(self):
        total = self.S[region(self.c)].astype(F32)
        for s in (1, 2, 3):
            self.ln.wait(self.g3.at[s - 1], dev(self.a1, (self.c[self.a1] + s) % 4), self.k3[s - 1])
            total = total + self.g3[s - 1].astype(F32)
        return total


def wide(refs, y, zh):
    return jnp.concatenate([r[y, zh].reshape(TOKENS, r.shape[-1]) for r in refs], axis=1)


def add_plane(total, x, v, axis, first, width, w, flipped):
    if axis == "x":
        tiles = [x[t // 2, t % 2, :, pl.ds(v, 1)].reshape(128, width) for t in range(8)]
        starts = [t * COLS + first for t in range(8)]
    elif axis == "y":
        tiles = [x[v, zh].reshape(TOKENS, width) for zh in range(2)]
        starts = [pl.multiple_of((v * 2 + zh) * COLS + first, 128) for zh in range(2)]
    else:
        tiles = [x[y, v // 2, :, :, pl.ds(v % 2, 1)].reshape(256, width) for y in range(4)]
        starts = [pl.multiple_of((y * 2 + v // 2) * COLS + first, 128) for y in range(4)]
    lhs = jnp.concatenate(tiles, axis=1)
    if flipped:
        rhs = jnp.concatenate([w[pl.ds(2 * HID, SHID), pl.ds(a, width)] for a in starts], axis=1)
        part = lax.dot_general(lhs, rhs, (((1,), (1,)), ((), ())), preferred_element_type=F32)
    else:
        rhs = jnp.concatenate([w[pl.ds(a, width)] for a in starts], axis=0)
        part = jnp.dot(lhs, rhs, preferred_element_type=F32)
    n = part.shape[-1]
    if axis == "x":
        total[:, pl.ds(v, 1)] += part.reshape(2, 1, 2, ROWS, n)
    elif axis == "y":
        total[...] += part.reshape(2, 4, 2, ROWS, n)
    else:
        total[:, :, pl.ds(v % 2, 1)] += part.reshape(2, 4, 1, ROWS, n)


def kernel(tok, ids_in, gw_in, tg, tu, td, sg, su, sd, gg, gu, gd, loss, *scratch):
    X, Dx, S, R1, R2, R3 = (scratch[3 * i : 3 * i + 3] for i in range(6))
    ids, gw, W, WD, acc, dacc, acts, stage, sact, dcat, wt, turned, lb, ss, rs, lsem = scratch[18:]
    c = coords()
    dp = c["dp"]
    other = {"dp": 1 - dp}
    expert = c["x"] * 2 + c["zl"]

    first_loads = [
        pltpu.make_async_copy(tok.at[:, pl.ds(first, width)], x.at[c["y"], c["zh"], dp, c["x"], c["zl"]], lsem.at[6 + n])
        for n, (x, (first, width, _)) in enumerate(zip(X, PARTS))
    ]
    first_loads.append(pltpu.make_async_copy(ids_in, ids, lsem.at[9]))
    first_loads.append(pltpu.make_async_copy(gw_in, gw, lsem.at[10]))
    loads = [
        pltpu.make_async_copy(tg.at[0], W.at[:, pl.ds(0, HID)], lsem.at[0]),
        pltpu.make_async_copy(tu.at[0], W.at[:, pl.ds(HID, HID)], lsem.at[1]),
        pltpu.make_async_copy(sg, W.at[:, pl.ds(2 * HID, SHID)], lsem.at[2]),
        pltpu.make_async_copy(su, W.at[:, pl.ds(2 * HID + SHID, SHID)], lsem.at[3]),
        pltpu.make_async_copy(td.at[0], WD.at[pl.ds(dp * HID, HID)], lsem.at[4]),
        pltpu.make_async_copy(sd, WD.at[pl.ds(2 * HID, SHID)], lsem.at[5]),
    ]

    for cp in first_loads + loads:
        cp.start()
    bar = pltpu.get_barrier_semaphore()
    for a in "xyz":
        for s in (1, 2, 3):
            pl.semaphore_signal(bar, inc=1, device_id=dev(a, (c[a] + s) % 4), device_id_type=MESH)
    pl.semaphore_signal(bar, inc=1, device_id=other, device_id_type=MESH)

    own = region(c, dp)
    acc[...] = jnp.zeros_like(acc)
    for cp in first_loads:
        cp.wait()
    norm = gw[...] / jnp.sum(gw[...], axis=0, keepdims=True)
    sub = lax.broadcasted_iota(jnp.int32, (8, ROWS), 0)
    turned[...] = jnp.zeros_like(turned)
    turned[0:8, 0:ROWS] = jnp.where(sub == ids[0:1], norm[0:1], 0.0) + jnp.where(sub == ids[1:2], norm[1:2], 0.0)
    weight = turned[...].T[0:ROWS]
    wt[pl.ds(dp, 1), pl.ds(c["x"], 1), pl.ds(c["zl"], 1)] = weight[None, None, None]

    pl.semaphore_wait(bar, 10)
    ln = Links(ss, rs)
    parts = [Gather(c, ln, x, axes) for x, (_, _, axes) in zip(X, PARTS)]
    for g in parts:
        g.start1()

    k_td, k_h, k_zl, k_wd = (ln.number() for _ in range(4))
    k_wx = [ln.number() for _ in range(3)]
    mine = wt.at[pl.ds(dp, 1), pl.ds(c["x"], 1), pl.ds(c["zl"], 1)]
    pair = wt.at[pl.ds(dp, 1), pl.ds(c["x"], 1)]
    ln.send(mine, mine, {"zl": 1 - c["zl"]}, k_zl)
    ln.send(td.at[0], WD.at[pl.ds(dp * HID, HID)], other, k_td)
    for g in parts:
        g.start2()
    ln.wait(wt.at[pl.ds(dp, 1), pl.ds(c["x"], 1), pl.ds(1 - c["zl"], 1)], {"zl": 1 - c["zl"]}, k_zl)
    for s in (1, 2, 3):
        ln.send(pair, pair, dev("x", (c["x"] + s) % 4), k_wx[s - 1])

    def up(i, v):
        while loads:
            loads.pop().wait()
        first, width, axes = PARTS[i]
        add_plane(acc, X[i], v, axes[2], first, width, W, False)

    gather_rest(parts, up)
    for s in (1, 2, 3):
        ln.wait(wt.at[pl.ds(dp, 1), pl.ds((c["x"] + 4 - s) % 4, 1)], dev("x", (c["x"] + s) % 4), k_wx[s - 1])
    ln.send(wt.at[pl.ds(dp, 1)], wt.at[pl.ds(dp, 1)], other, k_wd)
    ln.wait(wt.at[pl.ds(1 - dp, 1)], other, k_wd)

    lane = lax.broadcasted_iota(jnp.int32, (128, 128), 1)

    def act_step(i, carry):
        half = (1 - dp + i // 2) % 2
        two = pl.ds((i % 2) * 2, 2)
        w4 = wt[half, two].reshape(128, 128)
        w = jnp.sum(jnp.where(lane == expert, w4, 0.0), axis=1, keepdims=True)

        def cols(a, n):
            return acc[half, two, :, :, a : a + n].reshape(128, n)

        g, u = cols(0, HID), cols(HID, HID)
        h = (g * jax.nn.sigmoid(g) * u * (-w)).astype(BF16)
        to = pl.ds(pl.multiple_of((i % 2) * 128, 128), 128)
        g, u = cols(2 * HID, SHID), cols(2 * HID + SHID, SHID)
        a = (g * jax.nn.sigmoid(g) * u).astype(BF16)
        sact[pl.ds(pl.multiple_of(half * 256 + (i % 2) * 128, 128), 128)] = a

        @pl.when(i < 2)
        def _():
            stage[to] = h

        @pl.when(i >= 2)
        def _():
            acts[to, pl.ds(pl.multiple_of(dp * HID, HID), HID)] = h
            acts[to, 2 * HID :] = a

        return carry

    lax.fori_loop(0, 2, act_step, 0)
    there = acts.at[:, pl.ds(pl.multiple_of(dp * HID, HID), HID)]
    ln.send(stage, there, other, k_h)
    lax.fori_loop(2, 4, act_step, 0)
    ln.wait(WD.at[pl.ds((1 - dp) * HID, HID)], other, k_td)
    ln.wait(acts.at[:, pl.ds(pl.multiple_of((1 - dp) * HID, HID), HID)], other, k_h)

    reduces = [Reduce(c, ln, *refs, axes) for *refs, (_, _, axes) in zip(S, R1, R2, R3, PARTS)]
    for n, (red, (first, width, _)) in enumerate(zip(reduces, PARTS)):
        for y in (0, 2):
            w = jnp.concatenate([WD[:, (2 * y + t) * COLS + first : (2 * y + t) * COLS + first + width] for t in range(4)], axis=1)
            part = jnp.dot(acts[...], w, preferred_element_type=F32).astype(BF16)
            for t in range(4):
                red.S[y + t // 2, t % 2] = part[:, t * width : (t + 1) * width].reshape(4, 2, ROWS, width)
        for k in range(4):
            red.ring1(k)
        if n == 1:
            reduces[0].ring2(0)

    def turn(y, carry):
        for zh in range(2):
            for x, (first, width, _) in zip(X, PARTS):
                rows = pl.ds(pl.multiple_of(y * 1280 + zh * COLS + first, 128), width)
                W[rows, 0:TOKENS] = x[y, zh].reshape(TOKENS, width).T
        return carry

    lax.fori_loop(0, 4, turn, 0)

    for k in range(5):
        for red in reduces:
            if k < 4 and not (k == 0 and red is reduces[0]):
                red.ring2(k)
        for red in reduces:
            if k > 0:
                red.ring3(k - 1)
    for red in reduces:
        red.second()
    grads = [Gather(c, ln, x, axes) for x, (_, _, axes) in zip(Dx, PARTS)]
    squares = jnp.zeros((8, 128), F32)
    for red, g, (_, width, _) in zip(reduces, grads, PARTS):
        res = red.third()
        g.X[own] = (res * (1.0 / math.sqrt(TOKENS))).astype(BF16)[:, :, None]
        g.start1()
        sq = res.reshape(4, 8, width)
        sq = jnp.sum(sq * sq, axis=0)
        for j in range(width // 128):
            squares = squares + sq[:, 128 * j : 128 * j + 128]

    def loss_send(n, axis, value):
        k = [ln.number() for _ in range(3)]
        lb[n, pl.ds(c[axis], 1)] = value[None]
        count = 2 if axis == "dp" else 4
        mine = lb.at[n, pl.ds(c[axis], 1)]
        peers = [(s, (c[axis] + s) % count, (c[axis] + count - s) % count) for s in range(1, count)]
        for s, to, _ in peers:
            ln.send(mine, mine, dev(axis, to), k[s - 1])
        return n, axis, peers, k

    def loss_wait(sent):
        n, axis, peers, k = sent
        for s, to, source in peers:
            ln.wait(lb.at[n, pl.ds(source, 1)], dev(axis, to), k[s - 1])
        total = lb[n, 0] + lb[n, 1]
        return total if axis == "dp" else total + lb[n, 2] + lb[n, 3]

    sent = loss_send(0, "x", squares)
    for g in grads:
        g.start2()
    sent = loss_send(1, "y", loss_wait(sent))

    stages = []

    def back(i, v):
        nonlocal sent
        first, width, axes = PARTS[i]
        if len(stages) == 0:
            sent = loss_send(2, "z", loss_wait(sent))
        if len(stages) == 3:
            sent = loss_send(3, "dp", loss_wait(sent))
        stages.append(i)
        add_plane(dacc, Dx[i], v, axes[2], first, width, WD, True)

    dacc[...] = jnp.zeros_like(dacc)
    gather_rest(grads, back)

    g, u = (acc[..., a : a + SHID].reshape(TOKENS, SHID) for a in (2 * HID, 2 * HID + SHID))
    da = dacc[...].reshape(TOKENS, SHID)
    s = jax.nn.sigmoid(g)
    dcat[:, 0:SHID] = (da * u * s * (1.0 + g * (1.0 - s))).astype(BF16)
    dcat[:, SHID:] = (da * g * s).astype(BF16)

    def grad_step(t, carry):
        rows = pl.ds(pl.multiple_of(t * COLS, 128), COLS)
        both = jnp.dot(W[rows, 0:TOKENS], dcat[...], preferred_element_type=F32).astype(BF16)
        gg[rows] = both[:, :SHID]
        gu[rows] = both[:, SHID:]
        d = wide(Dx, t // 2, t % 2)
        gd[:, rows] = lax.dot_general(
            sact[...], d, (((0,), (0,)), ((), ())), preferred_element_type=F32
        ).astype(BF16)
        return carry

    lax.fori_loop(0, 8, grad_step, 0)
    loss[...] = jnp.sum(loss_wait(sent), keepdims=True) / (TOKENS * D)
    ln.finish()


def placed(a, b, c, a_out, b_out, c_out, sems):
    copies = [pltpu.make_async_copy(*refs, sems.at[n]) for n, refs in enumerate(((a, a_out), (b, b_out), (c, c_out)))]
    for cp in copies:
        cp.start()
    for cp in copies:
        cp.wait()


def body(*args):
    vmem, hbm = pl.BlockSpec(memory_space=pltpu.VMEM), pl.BlockSpec(memory_space=pltpu.HBM)
    blocks = {"x": (1, 1, 4, 1), "y": (4, 1, 1, 1), "z": (1, 2, 1, 2)}
    whole = [pltpu.VMEM((4, 2, 2, 4, 2, ROWS, w), BF16) for _, w, _ in PARTS]
    gg, gu, gd, loss = pl.pallas_call(
        kernel,
        out_shape=(
            jax.ShapeDtypeStruct((D, SHID), BF16),
            jax.ShapeDtypeStruct((D, SHID), BF16),
            jax.ShapeDtypeStruct((SHID, D), BF16),
            jax.ShapeDtypeStruct((1, 1), F32),
        ),
        in_specs=[hbm] * 9,
        out_specs=(vmem,) * 4,
        scratch_shapes=[
            *whole,
            *whole,
            *[pltpu.VMEM((4, 2, 4, 2, ROWS, w), BF16) for _, w, _ in PARTS],
            *[pltpu.VMEM((4, 6, *blocks[a[0]], 16, w), BF16) for _, w, a in PARTS],
            *[pltpu.VMEM((3, *blocks[a[0]], ROWS, w), BF16) for _, w, a in PARTS],
            *[pltpu.VMEM((3, 1, 1, 1, 1, ROWS, w), BF16) for _, w, _ in PARTS],
            pltpu.VMEM((2, ROWS), jnp.int32),
            pltpu.VMEM((2, ROWS), F32),
            pltpu.VMEM((D, 2 * HID + 2 * SHID), BF16),
            pltpu.VMEM((2 * HID + SHID, D), BF16),
            pltpu.VMEM((2, 4, 2, ROWS, 2 * HID + 2 * SHID), F32),
            pltpu.VMEM((2, 4, 2, ROWS, SHID), F32),
            pltpu.VMEM((TOKENS // 2, 2 * HID + SHID), BF16),
            pltpu.VMEM((TOKENS // 2, HID), BF16),
            pltpu.VMEM((TOKENS, SHID), BF16),
            pltpu.VMEM((TOKENS, 2 * SHID), BF16),
            pltpu.VMEM((2, 4, 2, ROWS, 128), F32),
            pltpu.VMEM((128, 128), F32),
            pltpu.VMEM((4, 4, 8, 128), F32),
            pltpu.SemaphoreType.DMA((300,)),
            pltpu.SemaphoreType.DMA((300,)),
            pltpu.SemaphoreType.DMA((11,)),
        ],
        compiler_params=pltpu.CompilerParams(
            collective_id=0, has_side_effects=True, vmem_limit_bytes=50 * 2**20
        ),
    )(args[0], args[1].T, args[2].T, *args[3:])
    anywhere = pl.BlockSpec(memory_space=pl.ANY)
    gg, gu, gd = pl.pallas_call(
        placed,
        out_shape=tuple(jax.ShapeDtypeStruct(a.shape, BF16) for a in (gg, gu, gd)),
        in_specs=[anywhere] * 3,
        out_specs=(pl.BlockSpec(memory_space=pltpu.HBM),) * 3,
        scratch_shapes=[pltpu.SemaphoreType.DMA((3,))],
        compiler_params=pltpu.CompilerParams(vmem_limit_bytes=4 * 2**20),
    )(gg, gu, gd)
    return gg, gu, gd, loss[0, 0]


def solution(mesh):
    finer = Mesh(mesh.devices.reshape(2, 4, 2, 4, 2), AXES)
    rows, tensor, expert = ("dp", "x", "zl"), ("y", "zh"), ("x", "zl")
    hidden, shards = ("dp", "y", "zh"), ("x", "zl", "y", "zh")
    return jax.shard_map(
        body,
        mesh=finer,
        in_specs=(
            P(rows, tensor),
            P(rows, None),
            P(rows, None),
            P(expert, None, hidden),
            P(expert, None, hidden),
            P(expert, hidden, None),
            P(None, shards),
            P(None, shards),
            P(shards, None),
        ),
        out_specs=(P(None, shards), P(None, shards), P(shards, None), P()),
        check_vma=False,
    )
```

```python
import functools
import math

import jax
import jax.numpy as jnp
from jax import lax
from jax.experimental import pallas as pl
from jax.experimental.pallas import tpu as pltpu
from jax.sharding import Mesh
from jax.sharding import PartitionSpec as P

MESH = pl.DeviceIdType.MESH
AXES = ("dp", "x", "zl", "y", "zh")
D, ROWS, COLS, HID, SHID, TOKENS = 5120, 32, 640, 512, 128, 512
PARTS = ((0, 256, "yzx"), (256, 256, "zxy"), (512, 128, "xyz"))
GROUPS = (2, 3, 1, 0)
RECEIVES = 241
F32, BF16 = jnp.float32, jnp.bfloat16


def coords():
    c = {a: lax.axis_index(a) for a in AXES}
    c["z"] = c["zh"] * 2 + c["zl"]
    return c


def dev(axis, v):
    return {"zh": v // 2, "zl": v % 2} if axis == "z" else {axis: v}


def region(c, dp=None, rows=(0, ROWS), **fixed):
    at = {a: fixed.get(a, c[a]) for a in "xyz"}
    sl = {a: pl.ds(0, 4) if at[a] is None else pl.ds(at[a], 1) for a in "xy"}
    if at["z"] is None:
        zh = zl = pl.ds(0, 2)
    else:
        zh, zl = pl.ds(at["z"] // 2, 1), pl.ds(at["z"] % 2, 1)
    head = (sl["y"], zh) if dp is None else (sl["y"], zh, pl.ds(dp, 1))
    return (*head, sl["x"], zl, pl.ds(*rows))


class Links:
    def __init__(self, send_sem, recv_sem, filler):
        self.ss, self.rs, self.n = send_sem, recv_sem, 0
        self.filler, self.batch, self.tiles = filler, 0, 0

    def number(self):
        self.n += 1
        return self.n - 1

    def copy(self, src, dst, to, k):
        return pltpu.make_async_remote_copy(
            src_ref=src,
            dst_ref=dst,
            send_sem=self.ss.at[self.batch],
            recv_sem=self.rs.at[k],
            device_id=to,
            device_id_type=MESH,
        )

    def send(self, src, dst, to, k):
        self.copy(src, dst, to, k).start()
        self.tiles += math.prod(src.shape) * jnp.dtype(src.dtype).itemsize // 4096

    def wait(self, dst, to, k):
        self.copy(dst, dst, to, k).wait_recv()

    def taken(self):
        batch = self.batch, self.tiles
        self.batch, self.tiles = self.batch + 1, 0
        return batch

    def finish(self, batch):
        n, tiles = batch
        wide = max(b for b in range(1, 11) if tiles % b == 0)
        assert tiles // wide <= 320
        ref = self.filler.at[pl.ds(0, tiles // wide * 16), pl.ds(0, wide * 128)]
        pltpu.make_async_copy(ref, ref, self.ss.at[n]).wait()


class Gather:
    def __init__(self, c, links, X, axes):
        self.c, self.ln, self.X = c, links, X
        self.a1, self.a2, self.a3 = axes
        self.k1 = [links.number() for _ in range(3)]
        self.k2 = [links.number() for _ in range(3)]
        self.k3 = [[links.number() for _ in range(3)] for _ in range(4)]
        self.kd = [links.number() for _ in range(4)]
        self.r, self.l, self.o = (c[self.a3] + 1) % 4, (c[self.a3] + 3) % 4, (c[self.a3] + 2) % 4

    def at(self, rows=(0, ROWS), dp=None, **fixed):
        return self.X.at[region(self.c, self.c["dp"] if dp is None else dp, rows, **fixed)]

    def peer(self, axis, s):
        return dev(axis, (self.c[axis] + s) % 4)

    def start1(self):
        for s in (1, 3, 2):
            self.ln.send(self.at(), self.at(), self.peer(self.a1, s), self.k1[s - 1])

    def start2(self):
        c = self.c
        for s in (1, 2, 3):
            self.ln.wait(self.at(**{self.a1: (c[self.a1] + 4 - s) % 4}), self.peer(self.a1, s), self.k1[s - 1])
        for s in (1, 3, 2):
            ref = self.at(**{self.a1: None})
            self.ln.send(ref, ref, self.peer(self.a2, s), self.k2[s - 1])
        self.ring1(0)

    def block(self, k, v3, rows=(0, ROWS)):
        return self.at(rows, **{self.a1: None, self.a2: (self.c[self.a2] + 4 - k) % 4, self.a3: v3})

    def ring1(self, k):
        if k:
            self.ln.wait(self.block(k, self.c[self.a3]), self.peer(self.a2, k), self.k2[k - 1])
        ref = self.block(k, self.c[self.a3])
        self.ln.send(ref, ref, dev(self.a3, self.r), self.k3[k][0])
        self.ln.send(ref, ref, dev(self.a3, self.l), self.k3[k][1])

    def ring2(self, k):
        self.ln.wait(self.block(k, self.l), dev(self.a3, self.r), self.k3[k][0])
        ref = self.block(k, self.l, (0, 16))
        self.ln.send(ref, ref, dev(self.a3, self.r), self.k3[k][2])
        self.ln.wait(self.block(k, self.r), dev(self.a3, self.l), self.k3[k][1])
        ref = self.block(k, self.r, (16, 16))
        self.ln.send(ref, ref, dev(self.a3, self.l), self.k3[k][2])

    def ring3(self, k):
        ref = self.block(k, self.o)
        self.ln.wait(ref, dev(self.a3, self.r), self.k3[k][2])
        self.ln.send(ref, ref, {"dp": 1 - self.c["dp"]}, self.kd[2])

    def plane(self, s, dp=None):
        return self.at(dp=dp, **{self.a1: None, self.a2: None, self.a3: (self.c[self.a3] + s) % 4})

    def across(self, s):
        self.ln.send(self.plane(s), self.plane(s), {"dp": 1 - self.c["dp"]}, self.kd[s])

    def crossed(self, s):
        dp = 1 - self.c["dp"]
        self.ln.wait(self.plane(s, dp), {"dp": dp}, self.kd[s])
        return (self.c[self.a3] + s) % 4


def gather_rest(parts, use):
    for g in parts:
        g.ring2(0)
    for k in (1, 3, 2):
        for g in parts:
            g.ring1(k)
    for g in parts:
        g.across(0)
    for i in (0, 1):
        use(i, parts[i].crossed(0))
    for g in parts:
        g.ring2(1)
    use(2, parts[2].crossed(0))
    for g in parts:
        g.ring2(3)
    for g in parts:
        g.ring2(2)
        g.across(1)
        g.across(3)
    for i, g in enumerate(parts):
        use(i, g.crossed(1))
    for k in (0, 1, 3, 2):
        for g in parts:
            g.ring3(k)
    for s in (3, 2):
        for i, g in enumerate(parts):
            use(i, g.crossed(s))


class Reduce:
    def __init__(self, c, links, sums, got1, got2, got3, axes):
        self.c, self.ln, self.S, self.g1, self.g2, self.g3 = c, links, sums, got1, got2, got3
        self.a1, self.a2, self.a3 = axes
        self.k1 = [[links.number() for _ in range(6)] for _ in range(4)]
        self.k2 = [links.number() for _ in range(3)]
        self.k3 = [links.number() for _ in range(3)]
        self.r, self.l, self.o = (c[self.a3] + 1) % 4, (c[self.a3] + 3) % 4, (c[self.a3] + 2) % 4

    def idx(self, k, v3, rows=(0, ROWS)):
        v2 = self.c[self.a2] ^ GROUPS[k]
        return region(self.c, None, rows, **{self.a1: None, self.a2: v2, self.a3: v3})

    def right(self, k, j, src):
        self.ln.send(src, self.g1.at[k, j], dev(self.a3, self.r), self.k1[k][j])

    def left(self, k, j, src):
        self.ln.send(src, self.g1.at[k, j], dev(self.a3, self.l), self.k1[k][j])

    def got(self, k, j):
        self.ln.wait(self.g1.at[k, j], dev(self.a3, self.r if j < 3 else self.l), self.k1[k][j])
        return self.g1[k, j].astype(F32)

    def ring1(self, k):
        S = self.S
        self.right(k, 0, S.at[self.idx(k, self.o, (0, 16))])
        self.left(k, 3, S.at[self.idx(k, self.o, (16, 16))])
        self.right(k, 1, S.at[self.idx(k, self.r, (16, 16))])
        self.left(k, 4, S.at[self.idx(k, self.l, (0, 16))])

    def ring2(self, k):
        S = self.S
        i = self.idx(k, self.r, (0, 16))
        S[i] = (S[i].astype(F32) + self.got(k, 0)).astype(BF16)
        self.right(k, 2, S.at[i])
        i = self.idx(k, self.l, (16, 16))
        S[i] = (S[i].astype(F32) + self.got(k, 3)).astype(BF16)
        self.left(k, 5, S.at[i])

    def ring3(self, k):
        S, own = self.S, self.c[self.a3]
        i = self.idx(k, own, (0, 16))
        S[i] = (S[i].astype(F32) + self.got(k, 4) + self.got(k, 2)).astype(BF16)
        i = self.idx(k, own, (16, 16))
        S[i] = (S[i].astype(F32) + self.got(k, 1) + self.got(k, 5)).astype(BF16)
        s = GROUPS[k]
        if s:
            to = dev(self.a2, self.c[self.a2] ^ s)
            self.ln.send(S.at[self.idx(k, own)], self.g2.at[s - 1], to, self.k2[s - 1])

    def second(self):
        S = self.S
        i = region(self.c, **{self.a1: None})
        total = S[i].astype(F32)
        for s in (1, 2, 3):
            self.ln.wait(self.g2.at[s - 1], dev(self.a2, self.c[self.a2] ^ s), self.k2[s - 1])
            total = total + self.g2[s - 1].astype(F32)
        S[i] = total.astype(BF16)
        for s in (1, 3, 2):
            v1 = (self.c[self.a1] + s) % 4
            self.ln.send(S.at[region(self.c, **{self.a1: v1})], self.g3.at[s - 1], dev(self.a1, v1), self.k3[s - 1])

    def third(self):
        total = self.S[region(self.c)].astype(F32)
        for s in (1, 2, 3):
            self.ln.wait(self.g3.at[s - 1], dev(self.a1, (self.c[self.a1] + s) % 4), self.k3[s - 1])
            total = total + self.g3[s - 1].astype(F32)
        return total


def wide(refs, y, zh):
    return jnp.concatenate([r[y, zh].reshape(TOKENS, r.shape[-1]) for r in refs], axis=1)


def add_plane(total, x, v, axis, first, width, w, flipped):
    if axis == "x":
        tiles = [x[t // 2, t % 2, :, pl.ds(v, 1)].reshape(128, width) for t in range(8)]
        starts = [t * COLS + first for t in range(8)]
    elif axis == "y":
        tiles = [x[v, zh].reshape(TOKENS, width) for zh in range(2)]
        starts = [pl.multiple_of((v * 2 + zh) * COLS + first, 128) for zh in range(2)]
    else:
        tiles = [x[y, v // 2, :, :, pl.ds(v % 2, 1)].reshape(256, width) for y in range(4)]
        starts = [pl.multiple_of((y * 2 + v // 2) * COLS + first, 128) for y in range(4)]
    lhs = jnp.concatenate(tiles, axis=1)
    if flipped:
        rhs = jnp.concatenate([w[pl.ds(2 * HID, SHID), pl.ds(a, width)] for a in starts], axis=1)
        part = lax.dot_general(lhs, rhs, (((1,), (1,)), ((), ())), preferred_element_type=F32)
    else:
        rhs = jnp.concatenate([w[pl.ds(a, width)] for a in starts], axis=0)
        part = jnp.dot(lhs, rhs, preferred_element_type=F32)
    n = part.shape[-1]
    if axis == "x":
        total[:, pl.ds(v, 1)] += part.reshape(2, 1, 2, ROWS, n)
    elif axis == "y":
        total[...] += part.reshape(2, 4, 2, ROWS, n)
    else:
        total[:, :, pl.ds(v % 2, 1)] += part.reshape(2, 4, 1, ROWS, n)


def kernel(tok, ids_in, gw_in, tg, tu, td, sg, su, sd, gg, gu, gd, loss, *scratch):
    X, Dx, S, R1, R2, R3 = (scratch[3 * i : 3 * i + 3] for i in range(6))
    ids, gw, W, WD, acc, dacc, acts, stage, sact, dcat, wt, turned, lb, ss, rs, lsem = scratch[18:]
    c = coords()
    dp = c["dp"]
    other = {"dp": 1 - dp}
    expert = c["x"] * 2 + c["zl"]

    first_loads = [
        pltpu.make_async_copy(tok.at[:, pl.ds(first, width)], x.at[c["y"], c["zh"], dp, c["x"], c["zl"]], lsem.at[6 + n])
        for n, (x, (first, width, _)) in enumerate(zip(X, PARTS))
    ]
    first_loads.append(pltpu.make_async_copy(ids_in, ids, lsem.at[9]))
    first_loads.append(pltpu.make_async_copy(gw_in, gw, lsem.at[10]))
    loads = [
        pltpu.make_async_copy(tg.at[0], W.at[:, pl.ds(0, HID)], lsem.at[0]),
        pltpu.make_async_copy(tu.at[0], W.at[:, pl.ds(HID, HID)], lsem.at[1]),
        pltpu.make_async_copy(sg, W.at[:, pl.ds(2 * HID, SHID)], lsem.at[2]),
        pltpu.make_async_copy(su, W.at[:, pl.ds(2 * HID + SHID, SHID)], lsem.at[3]),
        pltpu.make_async_copy(td.at[0], WD.at[pl.ds(dp * HID, HID)], lsem.at[4]),
        pltpu.make_async_copy(sd, WD.at[pl.ds(2 * HID, SHID)], lsem.at[5]),
    ]

    for cp in first_loads + loads:
        cp.start()
    bar = pltpu.get_barrier_semaphore()
    for a in "xyz":
        for s in (1, 2, 3):
            pl.semaphore_signal(bar, inc=1, device_id=dev(a, (c[a] + s) % 4), device_id_type=MESH)
    pl.semaphore_signal(bar, inc=1, device_id=other, device_id_type=MESH)

    own = region(c, dp)
    acc[...] = jnp.zeros_like(acc)
    for cp in first_loads:
        cp.wait()
    norm = gw[...] / jnp.sum(gw[...], axis=0, keepdims=True)
    sub = lax.broadcasted_iota(jnp.int32, (8, ROWS), 0)
    turned[...] = jnp.zeros_like(turned)
    turned[0:8, 0:ROWS] = jnp.where(sub == ids[0:1], norm[0:1], 0.0) + jnp.where(sub == ids[1:2], norm[1:2], 0.0)
    weight = turned[...].T[0:ROWS]
    wt[pl.ds(dp, 1), pl.ds(c["x"], 1), pl.ds(c["zl"], 1)] = weight[None, None, None]

    pl.semaphore_wait(bar, 10)
    ln = Links(ss, rs, W)
    parts = [Gather(c, ln, x, axes) for x, (_, _, axes) in zip(X, PARTS)]
    for g in parts:
        g.start1()

    k_td, k_h, k_zl, k_wd = (ln.number() for _ in range(4))
    k_wx = [ln.number() for _ in range(3)]
    mine = wt.at[pl.ds(dp, 1), pl.ds(c["x"], 1), pl.ds(c["zl"], 1)]
    pair = wt.at[pl.ds(dp, 1), pl.ds(c["x"], 1)]
    ln.send(mine, mine, {"zl": 1 - c["zl"]}, k_zl)
    ln.send(td.at[0], WD.at[pl.ds(dp * HID, HID)], other, k_td)
    for g in parts:
        g.start2()
    ln.wait(wt.at[pl.ds(dp, 1), pl.ds(c["x"], 1), pl.ds(1 - c["zl"], 1)], {"zl": 1 - c["zl"]}, k_zl)
    for s in (1, 2, 3):
        ln.send(pair, pair, dev("x", (c["x"] + s) % 4), k_wx[s - 1])

    def up(i, v):
        while loads:
            loads.pop().wait()
        first, width, axes = PARTS[i]
        add_plane(acc, X[i], v, axes[2], first, width, W, False)

    gather_rest(parts, up)
    for s in (1, 2, 3):
        ln.wait(wt.at[pl.ds(dp, 1), pl.ds((c["x"] + 4 - s) % 4, 1)], dev("x", (c["x"] + s) % 4), k_wx[s - 1])
    ln.send(wt.at[pl.ds(dp, 1)], wt.at[pl.ds(dp, 1)], other, k_wd)
    ln.wait(wt.at[pl.ds(1 - dp, 1)], other, k_wd)

    lane = lax.broadcasted_iota(jnp.int32, (128, 128), 1)

    def act_step(i, carry):
        half = (1 - dp + i // 2) % 2
        two = pl.ds((i % 2) * 2, 2)
        w4 = wt[half, two].reshape(128, 128)
        w = jnp.sum(jnp.where(lane == expert, w4, 0.0), axis=1, keepdims=True)

        def cols(a, n):
            return acc[half, two, :, :, a : a + n].reshape(128, n)

        g, u = cols(0, HID), cols(HID, HID)
        h = (g * jax.nn.sigmoid(g) * u * (-w)).astype(BF16)
        to = pl.ds(pl.multiple_of((i % 2) * 128, 128), 128)
        g, u = cols(2 * HID, SHID), cols(2 * HID + SHID, SHID)
        a = (g * jax.nn.sigmoid(g) * u).astype(BF16)
        sact[pl.ds(pl.multiple_of(half * 256 + (i % 2) * 128, 128), 128)] = a

        @pl.when(i < 2)
        def _():
            stage[to] = h

        @pl.when(i >= 2)
        def _():
            acts[to, pl.ds(pl.multiple_of(dp * HID, HID), HID)] = h
            acts[to, 2 * HID :] = a

        return carry

    lax.fori_loop(0, 2, act_step, 0)
    there = acts.at[:, pl.ds(pl.multiple_of(dp * HID, HID), HID)]
    gathered = ln.taken()
    ln.send(stage, there, other, k_h)
    staged = ln.taken()
    lax.fori_loop(2, 4, act_step, 0)
    ln.wait(WD.at[pl.ds((1 - dp) * HID, HID)], other, k_td)
    ln.wait(acts.at[:, pl.ds(pl.multiple_of((1 - dp) * HID, HID), HID)], other, k_h)

    reduces = [Reduce(c, ln, *refs, axes) for *refs, (_, _, axes) in zip(S, R1, R2, R3, PARTS)]
    for n, (red, (first, width, _)) in enumerate(zip(reduces, PARTS)):
        for half in (0, 1):
            if n == 0:
                zh = (c["zh"] + 1 + half) % 2
                shards = [(y, zh) for y in range(4)]
            else:
                shards = [(2 * half + t // 2, t % 2) for t in range(4)]
            w = jnp.concatenate(
                [WD[:, pl.ds(pl.multiple_of((y * 2 + zh) * COLS + first, 128), width)] for y, zh in shards], axis=1
            )
            part = jnp.dot(acts[...], w, preferred_element_type=F32).astype(BF16)
            for t, (y, zh) in enumerate(shards):
                red.S[y, zh] = part[:, t * width : (t + 1) * width].reshape(4, 2, ROWS, width)
            if n == 0:
                red.ring1(2 * half)
                red.ring1(2 * half + 1)
        if n > 0:
            for k in range(4):
                red.ring1(k)
        if n == 1:
            reduces[0].ring2(0)

    def turn(y, carry):
        for zh in range(2):
            for x, (first, width, _) in zip(X, PARTS):
                rows = pl.ds(pl.multiple_of(y * 1280 + zh * COLS + first, 128), width)
                W[rows, 0:TOKENS] = x[y, zh].reshape(TOKENS, width).T
        return carry

    lax.fori_loop(0, 4, turn, 0)
    ln.finish(gathered)
    ln.finish(staged)

    for k in range(5):
        for red in reduces:
            if k < 4 and not (k == 0 and red is reduces[0]):
                red.ring2(k)
        for red in reduces:
            if k > 0:
                red.ring3(k - 1)
    for red in reduces:
        red.second()
    grads = [Gather(c, ln, x, axes) for x, (_, _, axes) in zip(Dx, PARTS)]
    reduced = ln.taken()
    squares = jnp.zeros((8, 128), F32)
    for red, g, (_, width, _) in zip(reduces, grads, PARTS):
        res = red.third()
        g.X[own] = (res * (1.0 / math.sqrt(TOKENS))).astype(BF16)[:, :, None]
        g.start1()
        sq = res.reshape(4, 8, width)
        sq = jnp.sum(sq * sq, axis=0)
        for j in range(width // 128):
            squares = squares + sq[:, 128 * j : 128 * j + 128]

    def loss_send(n, axis, value):
        k = [ln.number() for _ in range(3)]
        lb[n, pl.ds(c[axis], 1)] = value[None]
        count = 2 if axis == "dp" else 4
        mine = lb.at[n, pl.ds(c[axis], 1)]
        peers = [(s, (c[axis] + s) % count, (c[axis] + count - s) % count) for s in range(1, count)]
        for s, to, _ in peers:
            ln.send(mine, mine, dev(axis, to), k[s - 1])
        return n, axis, peers, k

    def loss_wait(sent):
        n, axis, peers, k = sent
        for s, to, source in peers:
            ln.wait(lb.at[n, pl.ds(source, 1)], dev(axis, to), k[s - 1])
        total = lb[n, 0] + lb[n, 1]
        return total if axis == "dp" else total + lb[n, 2] + lb[n, 3]

    sent = loss_send(0, "x", squares)
    for g in grads:
        g.start2()
    sent = loss_send(1, "y", loss_wait(sent))

    stages = []

    def back(i, v):
        nonlocal sent
        first, width, axes = PARTS[i]
        if len(stages) == 0:
            sent = loss_send(2, "z", loss_wait(sent))
            ln.finish(reduced)
        if len(stages) == 3:
            sent = loss_send(3, "dp", loss_wait(sent))
        stages.append(i)
        add_plane(dacc, Dx[i], v, axes[2], first, width, WD, True)

    dacc[...] = jnp.zeros_like(dacc)
    gather_rest(grads, back)

    g, u = (acc[..., a : a + SHID].reshape(TOKENS, SHID) for a in (2 * HID, 2 * HID + SHID))
    da = dacc[...].reshape(TOKENS, SHID)
    s = jax.nn.sigmoid(g)
    dcat[:, 0:SHID] = (da * u * s * (1.0 + g * (1.0 - s))).astype(BF16)
    dcat[:, SHID:] = (da * g * s).astype(BF16)

    def grad_step(t, carry):
        rows = pl.ds(pl.multiple_of(t * COLS, 128), COLS)
        both = jnp.dot(W[rows, 0:TOKENS], dcat[...], preferred_element_type=F32).astype(BF16)
        gg[rows] = both[:, :SHID]
        gu[rows] = both[:, SHID:]
        d = wide(Dx, t // 2, t % 2)
        gd[:, rows] = lax.dot_general(
            sact[...], d, (((0,), (0,)), ((), ())), preferred_element_type=F32
        ).astype(BF16)
        return carry

    lax.fori_loop(0, 8, grad_step, 0)
    loss[...] = jnp.sum(loss_wait(sent), keepdims=True) / (TOKENS * D)
    ln.finish(ln.taken())
    assert ln.n == RECEIVES and ln.batch == 4


def placed(a, b, c, a_out, b_out, c_out, sems):
    copies = [pltpu.make_async_copy(*refs, sems.at[n]) for n, refs in enumerate(((a, a_out), (b, b_out), (c, c_out)))]
    for cp in copies:
        cp.start()
    for cp in copies:
        cp.wait()


def body(*args):
    vmem, hbm = pl.BlockSpec(memory_space=pltpu.VMEM), pl.BlockSpec(memory_space=pltpu.HBM)
    blocks = {"x": (1, 1, 4, 1), "y": (4, 1, 1, 1), "z": (1, 2, 1, 2)}
    whole = [pltpu.VMEM((4, 2, 2, 4, 2, ROWS, w), BF16) for _, w, _ in PARTS]
    gg, gu, gd, loss = pl.pallas_call(
        kernel,
        out_shape=(
            jax.ShapeDtypeStruct((D, SHID), BF16),
            jax.ShapeDtypeStruct((D, SHID), BF16),
            jax.ShapeDtypeStruct((SHID, D), BF16),
            jax.ShapeDtypeStruct((1, 1), F32),
        ),
        in_specs=[hbm] * 9,
        out_specs=(vmem,) * 4,
        scratch_shapes=[
            *whole,
            *whole,
            *[pltpu.VMEM((4, 2, 4, 2, ROWS, w), BF16) for _, w, _ in PARTS],
            *[pltpu.VMEM((4, 6, *blocks[a[0]], 16, w), BF16) for _, w, a in PARTS],
            *[pltpu.VMEM((3, *blocks[a[0]], ROWS, w), BF16) for _, w, a in PARTS],
            *[pltpu.VMEM((3, 1, 1, 1, 1, ROWS, w), BF16) for _, w, _ in PARTS],
            pltpu.VMEM((2, ROWS), jnp.int32),
            pltpu.VMEM((2, ROWS), F32),
            pltpu.VMEM((D, 2 * HID + 2 * SHID), BF16),
            pltpu.VMEM((2 * HID + SHID, D), BF16),
            pltpu.VMEM((2, 4, 2, ROWS, 2 * HID + 2 * SHID), F32),
            pltpu.VMEM((2, 4, 2, ROWS, SHID), F32),
            pltpu.VMEM((TOKENS // 2, 2 * HID + SHID), BF16),
            pltpu.VMEM((TOKENS // 2, HID), BF16),
            pltpu.VMEM((TOKENS, SHID), BF16),
            pltpu.VMEM((TOKENS, 2 * SHID), BF16),
            pltpu.VMEM((2, 4, 2, ROWS, 128), F32),
            pltpu.VMEM((128, 128), F32),
            pltpu.VMEM((4, 4, 8, 128), F32),
            pltpu.SemaphoreType.DMA((4,)),
            pltpu.SemaphoreType.DMA((RECEIVES,)),
            pltpu.SemaphoreType.DMA((11,)),
        ],
        compiler_params=pltpu.CompilerParams(
            collective_id=0, has_side_effects=True, vmem_limit_bytes=50 * 2**20
        ),
    )(args[0], args[1].T, args[2].T, *args[3:])
    anywhere = pl.BlockSpec(memory_space=pl.ANY)
    gg, gu, gd = pl.pallas_call(
        placed,
        out_shape=tuple(jax.ShapeDtypeStruct(a.shape, BF16) for a in (gg, gu, gd)),
        in_specs=[anywhere] * 3,
        out_specs=(pl.BlockSpec(memory_space=pltpu.HBM),) * 3,
        scratch_shapes=[pltpu.SemaphoreType.DMA((3,))],
        compiler_params=pltpu.CompilerParams(vmem_limit_bytes=4 * 2**20),
    )(gg, gu, gd)
    return gg, gu, gd, loss[0, 0]


def solution(mesh):
    finer = Mesh(mesh.devices.reshape(2, 4, 2, 4, 2), AXES)
    rows, tensor, expert = ("dp", "x", "zl"), ("y", "zh"), ("x", "zl")
    hidden, shards = ("dp", "y", "zh"), ("x", "zl", "y", "zh")
    return jax.shard_map(
        body,
        mesh=finer,
        in_specs=(
            P(rows, tensor),
            P(rows, None),
            P(rows, None),
            P(expert, None, hidden),
            P(expert, None, hidden),
            P(expert, hidden, None),
            P(None, shards),
            P(None, shards),
            P(shards, None),
        ),
        out_specs=(P(None, shards), P(None, shards), P(shards, None), P()),
        check_vma=False,
    )
```

```python
import functools
import math

import jax
import jax.numpy as jnp
from jax import lax
from jax.experimental import pallas as pl
from jax.experimental.pallas import tpu as pltpu
from jax.sharding import Mesh
from jax.sharding import PartitionSpec as P

MESH = pl.DeviceIdType.MESH
AXES = ("dp", "x", "zl", "y", "zh")
D, ROWS, COLS, HID, SHID, TOKENS = 5120, 32, 640, 512, 128, 512
PARTS = ((0, 256, "yzx"), (256, 256, "zxy"), (512, 128, "xyz"))
GROUPS = (2, 3, 1, 0)
RECEIVES = 205
F32, BF16 = jnp.float32, jnp.bfloat16


def coords():
    c = {a: lax.axis_index(a) for a in AXES}
    c["z"] = c["zh"] * 2 + c["zl"]
    return c


def dev(axis, v):
    return {"zh": v // 2, "zl": v % 2} if axis == "z" else {axis: v}


def region(c, dp=None, rows=(0, ROWS), **fixed):
    at = {a: fixed.get(a, c[a]) for a in "xyz"}
    sl = {a: pl.ds(0, 4) if at[a] is None else pl.ds(at[a], 1) for a in "xy"}
    if at["z"] is None:
        zh = zl = pl.ds(0, 2)
    else:
        zh, zl = pl.ds(at["z"] // 2, 1), pl.ds(at["z"] % 2, 1)
    head = (sl["y"], zh) if dp is None else (sl["y"], zh, pl.ds(dp, 1))
    return (*head, sl["x"], zl, pl.ds(*rows))


class Links:
    def __init__(self, send_sem, recv_sem, filler):
        self.ss, self.rs, self.n = send_sem, recv_sem, 0
        self.filler, self.batch, self.tiles = filler, 0, 0

    def number(self):
        self.n += 1
        return self.n - 1

    def copy(self, src, dst, to, k):
        return pltpu.make_async_remote_copy(
            src_ref=src,
            dst_ref=dst,
            send_sem=self.ss.at[self.batch],
            recv_sem=self.rs.at[k],
            device_id=to,
            device_id_type=MESH,
        )

    def send(self, src, dst, to, k):
        self.copy(src, dst, to, k).start()
        self.tiles += math.prod(src.shape) * jnp.dtype(src.dtype).itemsize // 4096

    def wait(self, dst, to, k):
        self.copy(dst, dst, to, k).wait_recv()

    def taken(self):
        batch = self.batch, self.tiles
        self.batch, self.tiles = self.batch + 1, 0
        return batch

    def finish(self, batch):
        n, tiles = batch
        wide = max(b for b in range(1, 11) if tiles % b == 0)
        assert tiles // wide <= 320
        ref = self.filler.at[pl.ds(0, tiles // wide * 16), pl.ds(0, wide * 128)]
        pltpu.make_async_copy(ref, ref, self.ss.at[n]).wait()


class Gather:
    def __init__(self, c, links, X, axes):
        self.c, self.ln, self.X = c, links, X
        self.a1, self.a2, self.a3 = axes
        self.k1 = [links.number() for _ in range(3)]
        self.k2 = [links.number() for _ in range(3)]
        self.k3 = [[links.number() for _ in range(3)] for _ in range(4)]
        self.kd = [links.number() for _ in range(4)]
        self.r, self.l, self.o = (c[self.a3] + 1) % 4, (c[self.a3] + 3) % 4, (c[self.a3] + 2) % 4

    def at(self, rows=(0, ROWS), dp=None, **fixed):
        return self.X.at[region(self.c, self.c["dp"] if dp is None else dp, rows, **fixed)]

    def peer(self, axis, s):
        return dev(axis, (self.c[axis] + s) % 4)

    def start1(self):
        for s in (1, 3, 2):
            self.ln.send(self.at(), self.at(), self.peer(self.a1, s), self.k1[s - 1])

    def start2(self):
        c = self.c
        for s in (1, 2, 3):
            self.ln.wait(self.at(**{self.a1: (c[self.a1] + 4 - s) % 4}), self.peer(self.a1, s), self.k1[s - 1])
        for s in (1, 3, 2):
            ref = self.at(**{self.a1: None})
            self.ln.send(ref, ref, self.peer(self.a2, s), self.k2[s - 1])
        self.ring1(0)

    def block(self, k, v3, rows=(0, ROWS)):
        return self.at(rows, **{self.a1: None, self.a2: (self.c[self.a2] + 4 - k) % 4, self.a3: v3})

    def ring1(self, k):
        if k:
            self.ln.wait(self.block(k, self.c[self.a3]), self.peer(self.a2, k), self.k2[k - 1])
        ref = self.block(k, self.c[self.a3])
        self.ln.send(ref, ref, dev(self.a3, self.r), self.k3[k][0])
        self.ln.send(ref, ref, dev(self.a3, self.l), self.k3[k][1])

    def ring2(self, k):
        self.ln.wait(self.block(k, self.l), dev(self.a3, self.r), self.k3[k][0])
        ref = self.block(k, self.l, (0, 16))
        self.ln.send(ref, ref, dev(self.a3, self.r), self.k3[k][2])
        self.ln.wait(self.block(k, self.r), dev(self.a3, self.l), self.k3[k][1])
        ref = self.block(k, self.r, (16, 16))
        self.ln.send(ref, ref, dev(self.a3, self.l), self.k3[k][2])

    def ring3(self, k):
        ref = self.block(k, self.o)
        self.ln.wait(ref, dev(self.a3, self.r), self.k3[k][2])
        self.ln.send(ref, ref, {"dp": 1 - self.c["dp"]}, self.kd[2])

    def plane(self, s, dp=None):
        return self.at(dp=dp, **{self.a1: None, self.a2: None, self.a3: (self.c[self.a3] + s) % 4})

    def across(self, s):
        self.ln.send(self.plane(s), self.plane(s), {"dp": 1 - self.c["dp"]}, self.kd[s])

    def crossed(self, s):
        dp = 1 - self.c["dp"]
        self.ln.wait(self.plane(s, dp), {"dp": dp}, self.kd[s])
        return (self.c[self.a3] + s) % 4


def gather_rest(parts, use):
    for g in parts:
        g.ring2(0)
    for k in (1, 3, 2):
        for g in parts:
            g.ring1(k)
    for g in parts:
        g.across(0)
    for i in (0, 1):
        use(i, parts[i].crossed(0))
    for g in parts:
        g.ring2(1)
    use(2, parts[2].crossed(0))
    for g in parts:
        g.ring2(3)
    for g in parts:
        g.ring2(2)
        g.across(1)
        g.across(3)
    for i, g in enumerate(parts):
        use(i, g.crossed(1))
    for k in (0, 1, 3, 2):
        for g in parts:
            g.ring3(k)
    for s in (3, 2):
        for i, g in enumerate(parts):
            use(i, g.crossed(s))


class Reduce:
    def __init__(self, c, links, sums, got1, got2, got3, axes):
        self.c, self.ln, self.S, self.g1, self.g2, self.g3 = c, links, sums, got1, got2, got3
        self.a1, self.a2, self.a3 = axes
        first, second, third, fourth = ([links.number() for _ in range(4)] for _ in range(4))
        self.k1 = [[first[k], second[k], second[k], third[k], fourth[k], fourth[k]] for k in range(4)]
        self.k2, self.k3 = links.number(), links.number()
        self.r, self.l, self.o = (c[self.a3] + 1) % 4, (c[self.a3] + 3) % 4, (c[self.a3] + 2) % 4

    def idx(self, k, v3, rows=(0, ROWS)):
        v2 = self.c[self.a2] ^ GROUPS[k]
        return region(self.c, None, rows, **{self.a1: None, self.a2: v2, self.a3: v3})

    def right(self, k, j, src):
        self.ln.send(src, self.g1.at[k, j], dev(self.a3, self.r), self.k1[k][j])

    def left(self, k, j, src):
        self.ln.send(src, self.g1.at[k, j], dev(self.a3, self.l), self.k1[k][j])

    def arrived(self, k, j, n):
        self.ln.wait(self.g1.at[k, pl.ds(j, n)], dev(self.a3, self.r if j < 3 else self.l), self.k1[k][j])

    def got(self, k, j):
        return self.g1[k, j].astype(F32)

    def ring1(self, k):
        S = self.S
        self.right(k, 0, S.at[self.idx(k, self.o, (0, 16))])
        self.left(k, 3, S.at[self.idx(k, self.o, (16, 16))])
        self.right(k, 1, S.at[self.idx(k, self.r, (16, 16))])
        self.left(k, 4, S.at[self.idx(k, self.l, (0, 16))])

    def ring2(self, k):
        S = self.S
        i = self.idx(k, self.r, (0, 16))
        self.arrived(k, 0, 1)
        S[i] = (S[i].astype(F32) + self.got(k, 0)).astype(BF16)
        self.right(k, 2, S.at[i])
        i = self.idx(k, self.l, (16, 16))
        self.arrived(k, 3, 1)
        S[i] = (S[i].astype(F32) + self.got(k, 3)).astype(BF16)
        self.left(k, 5, S.at[i])

    def ring3(self, k):
        S, own = self.S, self.c[self.a3]
        self.arrived(k, 1, 2)
        self.arrived(k, 4, 2)
        i = self.idx(k, own, (0, 16))
        S[i] = (S[i].astype(F32) + self.got(k, 4) + self.got(k, 2)).astype(BF16)
        i = self.idx(k, own, (16, 16))
        S[i] = (S[i].astype(F32) + self.got(k, 1) + self.got(k, 5)).astype(BF16)
        s = GROUPS[k]
        if s:
            to = dev(self.a2, self.c[self.a2] ^ s)
            self.ln.send(S.at[self.idx(k, own)], self.g2.at[s - 1], to, self.k2)

    def second(self):
        S = self.S
        i = region(self.c, **{self.a1: None})
        total = S[i].astype(F32)
        self.ln.wait(self.g2, dev(self.a2, self.c[self.a2] ^ 1), self.k2)
        for s in (1, 2, 3):
            total = total + self.g2[s - 1].astype(F32)
        S[i] = total.astype(BF16)
        for s in (1, 3, 2):
            v1 = (self.c[self.a1] + s) % 4
            self.ln.send(S.at[region(self.c, **{self.a1: v1})], self.g3.at[s - 1], dev(self.a1, v1), self.k3)

    def third(self):
        total = self.S[region(self.c)].astype(F32)
        self.ln.wait(self.g3, dev(self.a1, (self.c[self.a1] + 1) % 4), self.k3)
        for s in (1, 2, 3):
            total = total + self.g3[s - 1].astype(F32)
        return total


def wide(refs, y, zh):
    return jnp.concatenate([r[y, zh].reshape(TOKENS, r.shape[-1]) for r in refs], axis=1)


def add_plane(total, x, v, axis, first, width, w, flipped):
    if axis == "x":
        tiles = [x[t // 2, t % 2, :, pl.ds(v, 1)].reshape(128, width) for t in range(8)]
        starts = [t * COLS + first for t in range(8)]
    elif axis == "y":
        tiles = [x[v, zh].reshape(TOKENS, width) for zh in range(2)]
        starts = [pl.multiple_of((v * 2 + zh) * COLS + first, 128) for zh in range(2)]
    else:
        tiles = [x[y, v // 2, :, :, pl.ds(v % 2, 1)].reshape(256, width) for y in range(4)]
        starts = [pl.multiple_of((y * 2 + v // 2) * COLS + first, 128) for y in range(4)]
    lhs = jnp.concatenate(tiles, axis=1)
    if flipped:
        rhs = jnp.concatenate([w[pl.ds(2 * HID, SHID), pl.ds(a, width)] for a in starts], axis=1)
        part = lax.dot_general(lhs, rhs, (((1,), (1,)), ((), ())), preferred_element_type=F32)
    else:
        rhs = jnp.concatenate([w[pl.ds(a, width)] for a in starts], axis=0)
        part = jnp.dot(lhs, rhs, preferred_element_type=F32)
    n = part.shape[-1]
    if axis == "x":
        total[:, pl.ds(v, 1)] += part.reshape(2, 1, 2, ROWS, n)
    elif axis == "y":
        total[...] += part.reshape(2, 4, 2, ROWS, n)
    else:
        total[:, :, pl.ds(v % 2, 1)] += part.reshape(2, 4, 1, ROWS, n)


def kernel(tok, ids_in, gw_in, tg, tu, td, sg, su, sd, gg, gu, gd, loss, *scratch):
    X, Dx, S, R1, R2, R3 = (scratch[3 * i : 3 * i + 3] for i in range(6))
    ids, gw, W, WD, acc, dacc, acts, stage, sact, dcat, wt, turned, lb, ss, rs, lsem = scratch[18:]
    c = coords()
    dp = c["dp"]
    other = {"dp": 1 - dp}
    expert = c["x"] * 2 + c["zl"]

    first_loads = [
        pltpu.make_async_copy(tok.at[:, pl.ds(first, width)], x.at[c["y"], c["zh"], dp, c["x"], c["zl"]], lsem.at[6 + n])
        for n, (x, (first, width, _)) in enumerate(zip(X, PARTS))
    ]
    first_loads.append(pltpu.make_async_copy(ids_in, ids, lsem.at[9]))
    first_loads.append(pltpu.make_async_copy(gw_in, gw, lsem.at[10]))
    loads = [
        pltpu.make_async_copy(tg.at[0], W.at[:, pl.ds(0, HID)], lsem.at[0]),
        pltpu.make_async_copy(tu.at[0], W.at[:, pl.ds(HID, HID)], lsem.at[1]),
        pltpu.make_async_copy(sg, W.at[:, pl.ds(2 * HID, SHID)], lsem.at[2]),
        pltpu.make_async_copy(su, W.at[:, pl.ds(2 * HID + SHID, SHID)], lsem.at[3]),
        pltpu.make_async_copy(td.at[0], WD.at[pl.ds(dp * HID, HID)], lsem.at[4]),
        pltpu.make_async_copy(sd, WD.at[pl.ds(2 * HID, SHID)], lsem.at[5]),
    ]

    for cp in first_loads + loads:
        cp.start()
    bar = pltpu.get_barrier_semaphore()
    for a in "xyz":
        for s in (1, 2, 3):
            pl.semaphore_signal(bar, inc=1, device_id=dev(a, (c[a] + s) % 4), device_id_type=MESH)
    pl.semaphore_signal(bar, inc=1, device_id=other, device_id_type=MESH)

    own = region(c, dp)
    acc[...] = jnp.zeros_like(acc)
    for cp in first_loads:
        cp.wait()
    norm = gw[...] / jnp.sum(gw[...], axis=0, keepdims=True)
    sub = lax.broadcasted_iota(jnp.int32, (8, ROWS), 0)
    turned[...] = jnp.zeros_like(turned)
    turned[0:8, 0:ROWS] = jnp.where(sub == ids[0:1], norm[0:1], 0.0) + jnp.where(sub == ids[1:2], norm[1:2], 0.0)
    weight = turned[...].T[0:ROWS]
    wt[pl.ds(dp, 1), pl.ds(c["x"], 1), pl.ds(c["zl"], 1)] = weight[None, None, None]

    pl.semaphore_wait(bar, 10)
    ln = Links(ss, rs, W)
    parts = [Gather(c, ln, x, axes) for x, (_, _, axes) in zip(X, PARTS)]
    for g in parts:
        g.start1()

    k_td, k_h, k_zl, k_wd = (ln.number() for _ in range(4))
    k_wx = [ln.number() for _ in range(3)]
    mine = wt.at[pl.ds(dp, 1), pl.ds(c["x"], 1), pl.ds(c["zl"], 1)]
    pair = wt.at[pl.ds(dp, 1), pl.ds(c["x"], 1)]
    ln.send(mine, mine, {"zl": 1 - c["zl"]}, k_zl)
    ln.send(td.at[0], WD.at[pl.ds(dp * HID, HID)], other, k_td)
    for g in parts:
        g.start2()
    ln.wait(wt.at[pl.ds(dp, 1), pl.ds(c["x"], 1), pl.ds(1 - c["zl"], 1)], {"zl": 1 - c["zl"]}, k_zl)
    for s in (1, 2, 3):
        ln.send(pair, pair, dev("x", (c["x"] + s) % 4), k_wx[s - 1])

    def up(i, v):
        while loads:
            loads.pop().wait()
        first, width, axes = PARTS[i]
        add_plane(acc, X[i], v, axes[2], first, width, W, False)

    gather_rest(parts, up)
    for s in (1, 2, 3):
        ln.wait(wt.at[pl.ds(dp, 1), pl.ds((c["x"] + 4 - s) % 4, 1)], dev("x", (c["x"] + s) % 4), k_wx[s - 1])
    ln.send(wt.at[pl.ds(dp, 1)], wt.at[pl.ds(dp, 1)], other, k_wd)
    ln.wait(wt.at[pl.ds(1 - dp, 1)], other, k_wd)

    lane = lax.broadcasted_iota(jnp.int32, (128, 128), 1)

    def act_step(i, carry):
        half = (1 - dp + i // 2) % 2
        two = pl.ds((i % 2) * 2, 2)
        w4 = wt[half, two].reshape(128, 128)
        w = jnp.sum(jnp.where(lane == expert, w4, 0.0), axis=1, keepdims=True)

        def cols(a, n):
            return acc[half, two, :, :, a : a + n].reshape(128, n)

        g, u = cols(0, HID), cols(HID, HID)
        h = (g * jax.nn.sigmoid(g) * u * (-w)).astype(BF16)
        to = pl.ds(pl.multiple_of((i % 2) * 128, 128), 128)
        g, u = cols(2 * HID, SHID), cols(2 * HID + SHID, SHID)
        a = (g * jax.nn.sigmoid(g) * u).astype(BF16)
        sact[pl.ds(pl.multiple_of(half * 256 + (i % 2) * 128, 128), 128)] = a

        @pl.when(i < 2)
        def _():
            stage[to] = h

        @pl.when(i >= 2)
        def _():
            acts[to, pl.ds(pl.multiple_of(dp * HID, HID), HID)] = h
            acts[to, 2 * HID :] = a

        return carry

    lax.fori_loop(0, 2, act_step, 0)
    there = acts.at[:, pl.ds(pl.multiple_of(dp * HID, HID), HID)]
    gathered = ln.taken()
    ln.send(stage, there, other, k_h)
    staged = ln.taken()
    lax.fori_loop(2, 4, act_step, 0)
    ln.wait(WD.at[pl.ds((1 - dp) * HID, HID)], other, k_td)
    ln.wait(acts.at[:, pl.ds(pl.multiple_of((1 - dp) * HID, HID), HID)], other, k_h)

    reduces = [Reduce(c, ln, *refs, axes) for *refs, (_, _, axes) in zip(S, R1, R2, R3, PARTS)]
    for n, (red, (first, width, _)) in enumerate(zip(reduces, PARTS)):
        for half in (0, 1):
            if n == 0:
                zh = (c["zh"] + 1 + half) % 2
                shards = [(y, zh) for y in range(4)]
            else:
                shards = [(2 * half + t // 2, t % 2) for t in range(4)]
            w = jnp.concatenate(
                [WD[:, pl.ds(pl.multiple_of((y * 2 + zh) * COLS + first, 128), width)] for y, zh in shards], axis=1
            )
            part = jnp.dot(acts[...], w, preferred_element_type=F32).astype(BF16)
            for t, (y, zh) in enumerate(shards):
                red.S[y, zh] = part[:, t * width : (t + 1) * width].reshape(4, 2, ROWS, width)
            if n == 0:
                red.ring1(2 * half)
                red.ring1(2 * half + 1)
        if n > 0:
            for k in range(4):
                red.ring1(k)
        if n == 1:
            reduces[0].ring2(0)

    def turn(y, carry):
        for zh in range(2):
            for x, (first, width, _) in zip(X, PARTS):
                rows = pl.ds(pl.multiple_of(y * 1280 + zh * COLS + first, 128), width)
                W[rows, 0:TOKENS] = x[y, zh].reshape(TOKENS, width).T
        return carry

    lax.fori_loop(0, 4, turn, 0)
    ln.finish(gathered)
    ln.finish(staged)

    for k in range(5):
        for red in reduces:
            if k < 4 and not (k == 0 and red is reduces[0]):
                red.ring2(k)
        for red in reduces:
            if k > 0:
                red.ring3(k - 1)
    for red in reduces:
        red.second()
    grads = [Gather(c, ln, x, axes) for x, (_, _, axes) in zip(Dx, PARTS)]
    reduced = ln.taken()
    squares = jnp.zeros((8, 128), F32)
    for red, g, (_, width, _) in zip(reduces, grads, PARTS):
        res = red.third()
        g.X[own] = (res * (1.0 / math.sqrt(TOKENS))).astype(BF16)[:, :, None]
        g.start1()
        sq = res.reshape(4, 8, width)
        sq = jnp.sum(sq * sq, axis=0)
        for j in range(width // 128):
            squares = squares + sq[:, 128 * j : 128 * j + 128]

    def loss_send(n, axis, value):
        k = [ln.number() for _ in range(3)]
        lb[n, pl.ds(c[axis], 1)] = value[None]
        count = 2 if axis == "dp" else 4
        mine = lb.at[n, pl.ds(c[axis], 1)]
        peers = [(s, (c[axis] + s) % count, (c[axis] + count - s) % count) for s in range(1, count)]
        for s, to, _ in peers:
            ln.send(mine, mine, dev(axis, to), k[s - 1])
        return n, axis, peers, k

    def loss_wait(sent):
        n, axis, peers, k = sent
        for s, to, source in peers:
            ln.wait(lb.at[n, pl.ds(source, 1)], dev(axis, to), k[s - 1])
        total = lb[n, 0] + lb[n, 1]
        return total if axis == "dp" else total + lb[n, 2] + lb[n, 3]

    sent = loss_send(0, "x", squares)
    for g in grads:
        g.start2()
    sent = loss_send(1, "y", loss_wait(sent))

    stages = []

    def back(i, v):
        nonlocal sent
        first, width, axes = PARTS[i]
        if len(stages) == 0:
            sent = loss_send(2, "z", loss_wait(sent))
            ln.finish(reduced)
        if len(stages) == 3:
            sent = loss_send(3, "dp", loss_wait(sent))
        stages.append(i)
        add_plane(dacc, Dx[i], v, axes[2], first, width, WD, True)

    dacc[...] = jnp.zeros_like(dacc)
    gather_rest(grads, back)

    g, u = (acc[..., a : a + SHID].reshape(TOKENS, SHID) for a in (2 * HID, 2 * HID + SHID))
    da = dacc[...].reshape(TOKENS, SHID)
    s = jax.nn.sigmoid(g)
    dcat[:, 0:SHID] = (da * u * s * (1.0 + g * (1.0 - s))).astype(BF16)
    dcat[:, SHID:] = (da * g * s).astype(BF16)

    def grad_step(t, carry):
        rows = pl.ds(pl.multiple_of(t * COLS, 128), COLS)
        both = jnp.dot(W[rows, 0:TOKENS], dcat[...], preferred_element_type=F32).astype(BF16)
        gg[rows] = both[:, :SHID]
        gu[rows] = both[:, SHID:]
        d = wide(Dx, t // 2, t % 2)
        gd[:, rows] = lax.dot_general(
            sact[...], d, (((0,), (0,)), ((), ())), preferred_element_type=F32
        ).astype(BF16)
        return carry

    lax.fori_loop(0, 8, grad_step, 0)
    loss[...] = jnp.sum(loss_wait(sent), keepdims=True) / (TOKENS * D)
    ln.finish(ln.taken())
    assert ln.n == RECEIVES and ln.batch == 4


def placed(a, b, c, a_out, b_out, c_out, sems):
    copies = [pltpu.make_async_copy(*refs, sems.at[n]) for n, refs in enumerate(((a, a_out), (b, b_out), (c, c_out)))]
    for cp in copies:
        cp.start()
    for cp in copies:
        cp.wait()


def body(*args):
    vmem, hbm = pl.BlockSpec(memory_space=pltpu.VMEM), pl.BlockSpec(memory_space=pltpu.HBM)
    blocks = {"x": (1, 1, 4, 1), "y": (4, 1, 1, 1), "z": (1, 2, 1, 2)}
    whole = [pltpu.VMEM((4, 2, 2, 4, 2, ROWS, w), BF16) for _, w, _ in PARTS]
    gg, gu, gd, loss = pl.pallas_call(
        kernel,
        out_shape=(
            jax.ShapeDtypeStruct((D, SHID), BF16),
            jax.ShapeDtypeStruct((D, SHID), BF16),
            jax.ShapeDtypeStruct((SHID, D), BF16),
            jax.ShapeDtypeStruct((1, 1), F32),
        ),
        in_specs=[hbm] * 9,
        out_specs=(vmem,) * 4,
        scratch_shapes=[
            *whole,
            *whole,
            *[pltpu.VMEM((4, 2, 4, 2, ROWS, w), BF16) for _, w, _ in PARTS],
            *[pltpu.VMEM((4, 6, *blocks[a[0]], 16, w), BF16) for _, w, a in PARTS],
            *[pltpu.VMEM((3, *blocks[a[0]], ROWS, w), BF16) for _, w, a in PARTS],
            *[pltpu.VMEM((3, 1, 1, 1, 1, ROWS, w), BF16) for _, w, _ in PARTS],
            pltpu.VMEM((2, ROWS), jnp.int32),
            pltpu.VMEM((2, ROWS), F32),
            pltpu.VMEM((D, 2 * HID + 2 * SHID), BF16),
            pltpu.VMEM((2 * HID + SHID, D), BF16),
            pltpu.VMEM((2, 4, 2, ROWS, 2 * HID + 2 * SHID), F32),
            pltpu.VMEM((2, 4, 2, ROWS, SHID), F32),
            pltpu.VMEM((TOKENS // 2, 2 * HID + SHID), BF16),
            pltpu.VMEM((TOKENS // 2, HID), BF16),
            pltpu.VMEM((TOKENS, SHID), BF16),
            pltpu.VMEM((TOKENS, 2 * SHID), BF16),
            pltpu.VMEM((2, 4, 2, ROWS, 128), F32),
            pltpu.VMEM((128, 128), F32),
            pltpu.VMEM((4, 4, 8, 128), F32),
            pltpu.SemaphoreType.DMA((4,)),
            pltpu.SemaphoreType.DMA((RECEIVES,)),
            pltpu.SemaphoreType.DMA((11,)),
        ],
        compiler_params=pltpu.CompilerParams(
            collective_id=0, has_side_effects=True, vmem_limit_bytes=50 * 2**20
        ),
    )(args[0], args[1].T, args[2].T, *args[3:])
    anywhere = pl.BlockSpec(memory_space=pl.ANY)
    gg, gu, gd = pl.pallas_call(
        placed,
        out_shape=tuple(jax.ShapeDtypeStruct(a.shape, BF16) for a in (gg, gu, gd)),
        in_specs=[anywhere] * 3,
        out_specs=(pl.BlockSpec(memory_space=pltpu.HBM),) * 3,
        scratch_shapes=[pltpu.SemaphoreType.DMA((3,))],
        compiler_params=pltpu.CompilerParams(vmem_limit_bytes=4 * 2**20),
    )(gg, gu, gd)
    return gg, gu, gd, loss[0, 0]


def solution(mesh):
    finer = Mesh(mesh.devices.reshape(2, 4, 2, 4, 2), AXES)
    rows, tensor, expert = ("dp", "x", "zl"), ("y", "zh"), ("x", "zl")
    hidden, shards = ("dp", "y", "zh"), ("x", "zl", "y", "zh")
    return jax.shard_map(
        body,
        mesh=finer,
        in_specs=(
            P(rows, tensor),
            P(rows, None),
            P(rows, None),
            P(expert, None, hidden),
            P(expert, None, hidden),
            P(expert, hidden, None),
            P(None, shards),
            P(None, shards),
            P(shards, None),
        ),
        out_specs=(P(None, shards), P(None, shards), P(shards, None), P()),
        check_vma=False,
    )
```
